32 devices in a mesh: band: 4 (over y, x), strip: 8 (over z, core).
Axes of the slice: x: 2, y: 2, z: 4, core: 2. Of those that a mesh axis runs over, the one named last changes fastest.
Arguments:
- cloud_field: bfloat16 [256, 256, 512], P('band', 'strip'), may hold values from -6 to 6
- row_gain: float32 [512], replicated, may hold values from 0.1 to 1.9
- row_qkv: bfloat16 [512, 1536], replicated, may hold values from -0.25 to 0.25
- row_out: bfloat16 [512, 512], replicated, may hold values from -1 to 1
- col_gain: float32 [512], replicated, may hold values from 0.1 to 1.9
- col_qkv: bfloat16 [512, 1536], replicated, may hold values from -0.25 to 0.25
- col_out: bfloat16 [512, 512], replicated, may hold values from -1 to 1
- plant_cell: int32 [4096], P(('band', 'strip')), may hold values from 0 to 2047
- plant_decoder_device: int32 [4096, 1], P(('band', 'strip')), may hold values from 0 to 31; in each aligned block of 128 rows (0 to 127, 128 to 255, ...) at most 8 rows name the same one
- plant_capacity: int32 [4096], P(('band', 'strip')), may hold values from 100 to 5000
- decode_first: bfloat16 [16384, 512], P(('band', 'strip')), may hold values from -0.25 to 0.25
- decode_second: bfloat16 [32, 512], P(('band', 'strip')), may hold values from -0.25 to 0.25
Outputs:
- final_field: bfloat16 [256, 256, 512], P('band', 'strip')
- plant_power: float32 [4096], P(('band', 'strip'))
- fleet_yield: float32 [], replicated
The draws below stay inside these ranges and needn't reach their ends.
Inputs may be any that keep to these rules, and one draw needn't show every extreme that they name: `plant_decoder_device`: among the 128 plants listed on one device, no owner is named more than 8 times.
All inputs are finite; a program needn't handle non-finite values.
Results may differ from the reference program's by a relative error of at most 0.015.
Values may be sent and summed in bfloat16 or wider, within the bound.
A program may use at most 64 MiB of HBM per device.

```python
import math
import jax
import jax.numpy as jnp
import numpy as np
from jax import lax

D = 512
HEADS = 8
DEC = 512
ROWS_DEV = 64
COLS_DEV = 32
PLANT_DEV = 128
TOK_DEV = 2048
H = 256
W = 256
OWNERS = 32
MOST = 8
PLANTS = 4096
N_STRIP = 8


def draw_plant_capacity(key, part):
    base = jax.random.randint(key, (PLANTS,), 100, 1001).astype(jnp.int32)
    device_of = jnp.arange(PLANTS, dtype=jnp.int32) // PLANT_DEV
    factor = (OWNERS + 4 * device_of).astype(jnp.int32)
    return (base * factor // OWNERS).astype(jnp.int32)


def touch_ends(values, stream_key, smallest, top_value):
    index_at = [jax.random.randint(jax.random.fold_in(stream_key, axis), (), 0, length) for axis, length in enumerate(values.shape)]
    main_axis = values.shape.index(max(values.shape))
    neighbour = index_at[:main_axis] + [(index_at[main_axis] + 1) % values.shape[main_axis]] + index_at[main_axis + 1:]
    return values.at[tuple(index_at)].set(smallest).at[tuple(neighbour)].set(top_value)


def shard_levels(rng, extent, pieces, smallest, largest):
    factor_of = 1.0
    for position, blocks in pieces:
        draws = jax.random.uniform(jax.random.fold_in(jax.random.fold_in(rng, 6), position), (blocks,), jnp.float32, smallest / len(pieces), largest / len(pieces))
        factor_of = factor_of * jnp.repeat(jnp.exp(draws), extent[position] // blocks).reshape((-1,) + (1,) * (len(extent) - 1 - position))
    return factor_of


def assign_block(own_key, own, number, rows, number_of, top, reach, slope):
    order = jax.random.permutation(own_key, number_of)
    packed, ordinary = shares(number_of, rows * top, reach, slope, True), shares(number_of, rows * top, reach, slope, False)
    places = jnp.arange(number_of)

    def named(tallies, turn):
        used = int((tallies > 0).sum())
        fixed = max(1, used // 4)
        passed = fixed + (places - fixed + turn * (used - fixed)) % max(1, number_of - fixed)
        return jnp.zeros((number_of,), jnp.int32).at[order[jnp.where(places < fixed, places, passed)]].set(jnp.asarray(tallies, jnp.int32))

    tallies = jnp.where(number % 4 == 0, named(packed, number // 4), named(ordinary, number - number // 4 - 1))
    mixed = jax.random.permutation(jax.random.fold_in(own, 3), number_of)
    donor, receiver = mixed[0:number_of // 2 * 2:2], mixed[1:number_of // 2 * 2:2]
    margin = jnp.minimum(tallies[donor] - 1, reach - tallies[receiver]) // 2
    margin = jnp.where((donor == order[0]) | (receiver == order[0]) | (tallies[receiver] == 0), 0, jnp.maximum(margin, 0))
    passed = jax.random.randint(jax.random.fold_in(own, 4), (number_of // 2,), 0, 1 << 20) % (margin + 1)
    tallies = tallies.at[donor].add(-passed).at[receiver].add(passed)
    labels = jnp.searchsorted(jnp.cumsum(tallies), jnp.arange(rows * top), side="right").astype(jnp.int32)
    table = labels.reshape(top, rows).T
    table = table[jax.random.permutation(jax.random.fold_in(own, 1), rows)]
    turn = jax.random.randint(jax.random.fold_in(own, 2), (rows, 1), 0, top)
    return jnp.take_along_axis(table, (jnp.arange(top)[None, :] + turn) % top, axis=1)


def shares(count, total, bound, slope, full):
    portions = [(1 << 20) // math.isqrt(grade ** slope) + 1 for grade in range(1, count + 1)]
    largest = bound if full else min(bound, max(-(-total // count), total * portions[0] // sum(portions)))
    least = 1 if total - largest >= count - 1 else 0
    given, spare = [largest] + [least] * (count - 1), total - largest - least * (count - 1)
    while spare > 0:
        movable = [i for i in range(1, count) if given[i] < largest] or [i for i in range(1, count) if given[i] < bound]
        whole, left = sum([portions[i] for i in movable]), spare
        for i in movable:
            extra = min(bound - given[i], max(1, left * portions[i] // whole), spare)
            given[i] = given[i] + extra
            spare = spare - extra
    return np.array(given)


def normal_values(own_key, shape, scale, most, split=(), kind=jnp.bfloat16):
    drawn = jax.random.normal(own_key, shape, jnp.float32) * scale
    if len(split) > 0:
        drawn = shard_levels(own_key, shape, split, -0.22, 0.18) * drawn
    return jnp.clip(drawn, min=-most, max=most).astype(kind)


def setup_inputs(seed: int = 0) -> dict:
    key_list = jax.random.split(jax.random.key(seed), 13)
    cloud_field = normal_values(key_list[0], (H, W, D), 1.0, 6.0, ((0, 4), (1, 8)))
    row_gain = jnp.clip(1.0 + 0.18 * jax.random.normal(key_list[1], (D,), jnp.float32), 0.1, 1.9)
    row_qkv = normal_values(key_list[2], (D, 3 * D), D ** -0.5, 0.25)
    row_out = normal_values(key_list[3], (D, D), (D // 16) ** -0.5, 1.0)
    col_gain = jnp.clip(1.0 + 0.18 * jax.random.normal(key_list[4], (D,), jnp.float32), 0.1, 1.9)
    col_qkv = normal_values(key_list[5], (D, 3 * D), D ** -0.5, 0.25)
    col_out = normal_values(key_list[6], (D, D), (D // 16) ** -0.5, 1.0)
    plant_cell = touch_ends(jax.random.randint(key_list[7], (PLANTS,), 0, TOK_DEV), jax.random.fold_in(key_list[7], 1), 0, TOK_DEV - 1).astype(jnp.int32)
    plant_decoder_device_keys = jax.random.split(jax.random.fold_in(key_list[8], 1), PLANTS // PLANT_DEV)
    plant_decoder_device_turns = jax.random.permutation(jax.random.fold_in(key_list[8], 3), PLANTS // PLANT_DEV)
    plant_decoder_device = jax.vmap(lambda own, number: assign_block(jax.random.fold_in(key_list[8], 2), own, number, PLANT_DEV, OWNERS, 1, MOST, 2))(plant_decoder_device_keys, plant_decoder_device_turns).reshape((PLANTS, 1))
    plant_capacity = draw_plant_capacity(jax.random.fold_in(key_list[12], 71), 0)
    decode_first = normal_values(key_list[10], (OWNERS * D, DEC), D ** -0.5, 0.25, ((0, 32),))
    decode_second = normal_values(key_list[11], (OWNERS, DEC), DEC ** -0.5, 0.25, ((0, 32),))
    return dict(cloud_field=cloud_field, row_gain=row_gain, row_qkv=row_qkv, row_out=row_out, col_gain=col_gain, col_qkv=col_qkv, col_out=col_out, plant_cell=plant_cell, plant_decoder_device=plant_decoder_device, plant_capacity=plant_capacity, decode_first=decode_first, decode_second=decode_second)


EPS = 1e-06
TAU = 12.0

def norm_rows(values, scale_factor):
    widened = values.astype(jnp.float32)
    return widened * lax.rsqrt(lax.optimization_barrier(jnp.mean(widened * widened, axis=-1, keepdims=True)) + EPS) * scale_factor.astype(jnp.float32)

def heads_norm(values):
    leading = values.shape[:-1]
    split_up = values.reshape(leading + (HEADS, values.shape[-1] // HEADS))
    normed = split_up * lax.rsqrt(lax.optimization_barrier(jnp.mean(split_up * split_up, axis=-1, keepdims=True)) + EPS)
    return normed.reshape(values.shape)

def project(tokens_in, scale_factor, weight_qkv):
    leading = tokens_in.shape[:-1]
    model_width = tokens_in.shape[-1]
    head_width = model_width // HEADS
    normed = norm_rows(tokens_in, scale_factor).astype(jnp.bfloat16).reshape(-1, model_width)
    projected = jnp.dot(normed, weight_qkv, preferred_element_type=jnp.float32)
    query = heads_norm(projected[:, :model_width]) * (TAU / head_width)
    keys_part = heads_norm(projected[:, model_width:2 * model_width])
    values_part = projected[:, 2 * model_width:]
    shaped = leading + (model_width,)
    return (query.astype(jnp.bfloat16).reshape(shaped), keys_part.astype(jnp.bfloat16).reshape(shaped), values_part.astype(jnp.bfloat16).reshape(shaped))

def attend(query, keys_part, values_part):
    batch_size, length, model_width = query.shape
    head_width = model_width // HEADS

    def split_heads(tensor):
        return tensor.reshape(batch_size, length, HEADS, head_width).transpose(2, 0, 1, 3)

    def one_head(operands):
        query_rows, key_rows, value_rows = operands
        attention_scores = jnp.einsum('zxe,zle->zxl', query_rows.astype(jnp.float32), key_rows.astype(jnp.float32))
        weights = jnp.exp(attention_scores)
        row_total = lax.optimization_barrier(jnp.sum(weights, axis=-1, keepdims=True))
        weights_bfloat = (weights / row_total).astype(jnp.bfloat16)
        return jnp.einsum('pem,pmj->pej', weights_bfloat.astype(jnp.float32), value_rows.astype(jnp.float32)).astype(jnp.bfloat16)
    context = lax.map(one_head, (split_heads(query), split_heads(keys_part), split_heads(values_part)))
    return context.transpose(1, 2, 0, 3).reshape(batch_size, length, model_width)

def finish(tokens_in, context, weight_out):
    model_width = tokens_in.shape[-1]
    mixed = jnp.dot(context.reshape(-1, model_width), weight_out, preferred_element_type=jnp.float32)
    return (tokens_in.astype(jnp.float32) + mixed.reshape(tokens_in.shape)).astype(jnp.bfloat16)

def mix_layer(tokens_in, scale_factor, weight_qkv, weight_out):
    query, keys_part, values_part = project(tokens_in, scale_factor, weight_qkv)
    return finish(tokens_in, attend(query, keys_part, values_part), weight_out)

def reference(cloud_field, row_gain, row_qkv, row_out, col_gain, col_qkv, col_out, plant_cell, plant_decoder_device, plant_capacity, decode_first, decode_second):
    rows_all, cols_all, model_width = cloud_field.shape
    row_blocks = cloud_field.reshape(rows_all // 8, 8, cols_all, model_width)
    after_rows = lax.map(lambda rows_block: mix_layer(rows_block, row_gain, row_qkv, row_out), row_blocks)
    after_rows = after_rows.reshape(rows_all, cols_all, model_width)
    col_blocks = after_rows.transpose(1, 0, 2).reshape(cols_all // 8, 8, rows_all, model_width)
    after_cols = lax.map(lambda cols_block: mix_layer(cols_block, col_gain, col_qkv, col_out), col_blocks)
    final_field = after_cols.reshape(cols_all, rows_all, model_width).transpose(1, 0, 2)
    device_of = jnp.arange(PLANTS, dtype=jnp.int32) // PLANT_DEV
    band_of = device_of // N_STRIP
    strip_of = device_of % N_STRIP
    row_of = (band_of * ROWS_DEV + plant_cell // COLS_DEV).astype(jnp.int32)
    col_of = (strip_of * COLS_DEV + plant_cell % COLS_DEV).astype(jnp.int32)
    features = final_field[row_of, col_of]
    owners = plant_decoder_device[:, 0]
    owner_grid = owners.reshape(OWNERS, PLANT_DEV)
    one_hot = (owner_grid[:, :, None] == jnp.arange(OWNERS, dtype=jnp.int32)[None, None, :]).astype(jnp.int32)
    running = jnp.cumsum(one_hot, axis=1).astype(jnp.int32)
    slot_of = lax.optimization_barrier(jnp.sum(one_hot * (running - 1), axis=2)).astype(jnp.int32).reshape(PLANTS)
    token_position = (owners * (OWNERS * MOST) + device_of * MOST + slot_of).astype(jnp.int32)
    table = jnp.zeros((OWNERS * OWNERS * MOST, model_width), jnp.bfloat16).at[token_position].set(features)
    table = table.reshape(OWNERS, OWNERS * MOST, model_width)
    first_parts = decode_first.reshape(OWNERS, model_width, DEC)

    def decode_owner(operands):
        slots_in, first_part, second_part = operands
        hidden = jax.nn.gelu(jnp.dot(slots_in, first_part, preferred_element_type=jnp.float32)).astype(jnp.bfloat16)
        return jax.nn.softplus(jnp.dot(hidden.astype(jnp.float32), second_part.astype(jnp.float32)))
    yields = lax.map(decode_owner, (table, first_parts, decode_second)).reshape(-1)
    capacity_w = plant_capacity.astype(jnp.float32) * 0.001
    plant_power = capacity_w * yields[token_position]
    fleet_yield = jnp.sum(plant_power) / float(PLANTS)
    return (final_field, plant_power, fleet_yield)
```

```python
import jax
import jax.numpy as jnp
from jax import lax
from jax.experimental import pallas as pl
from jax.experimental.pallas import tpu as pltpu
from jax.sharding import PartitionSpec as P

HEADS = 8


EPS = 1e-06
TAU = 12.0


def norm_rows(values, scale_factor):
    widened = values.astype(jnp.float32)
    return (
        widened
        * lax.rsqrt(jnp.mean(widened * widened, axis=-1, keepdims=True) + EPS)
        * scale_factor
    )


def heads_norm(values):
    leading = values.shape[:-1]
    split_up = values.reshape(leading + (HEADS, values.shape[-1] // HEADS))
    normed = split_up * lax.rsqrt(jnp.mean(split_up * split_up, axis=-1, keepdims=True) + EPS)
    return normed.reshape(values.shape)


def project(tokens_in, scale_factor, weight_qkv):
    leading = tokens_in.shape[:-1]
    model_width = tokens_in.shape[-1]
    head_width = model_width // HEADS
    normed = norm_rows(tokens_in, scale_factor).astype(jnp.bfloat16).reshape(-1, model_width)
    projected = jnp.dot(normed, weight_qkv, preferred_element_type=jnp.float32)
    query = heads_norm(projected[:, :model_width]) * (TAU / head_width)
    keys_part = heads_norm(projected[:, model_width : 2 * model_width])
    values_part = projected[:, 2 * model_width :]
    shaped = leading + (model_width,)
    return (
        query.astype(jnp.bfloat16).reshape(shaped),
        keys_part.astype(jnp.bfloat16).reshape(shaped),
        values_part.astype(jnp.bfloat16).reshape(shaped),
    )


def attend(query, keys_part, values_part):
    batch_size, length, model_width = query.shape
    head_width = model_width // HEADS

    def split_heads(tensor):
        return tensor.reshape(batch_size, length, HEADS, head_width).transpose(2, 0, 1, 3)

    def one_head(operands):
        query_rows, key_rows, value_rows = operands
        attention_scores = jnp.einsum(
            "zxe,zle->zxl", query_rows, key_rows, preferred_element_type=jnp.float32
        )
        weights = jnp.exp(attention_scores)
        row_total = jnp.sum(weights, axis=-1, keepdims=True)
        weights_bfloat = (weights / row_total).astype(jnp.bfloat16)
        return jnp.einsum(
            "pem,pmj->pej", weights_bfloat, value_rows, preferred_element_type=jnp.float32
        ).astype(jnp.bfloat16)

    context = lax.map(
        one_head, (split_heads(query), split_heads(keys_part), split_heads(values_part))
    )
    return context.transpose(1, 2, 0, 3).reshape(batch_size, length, model_width)


def finish(tokens_in, context, weight_out):
    model_width = tokens_in.shape[-1]
    mixed = jnp.dot(
        context.reshape(-1, model_width), weight_out, preferred_element_type=jnp.float32
    )
    return (tokens_in.astype(jnp.float32) + mixed.reshape(tokens_in.shape)).astype(jnp.bfloat16)


def mix_layer(tokens_in, scale_factor, weight_qkv, weight_out):
    query, keys_part, values_part = project(tokens_in, scale_factor, weight_qkv)
    return finish(tokens_in, attend(query, keys_part, values_part), weight_out)


def sequence_layer(x, gain, weight_qkv, weight_out, head_sum):
    length, width = x.shape
    head = width // HEADS
    pair = 2 * head
    scale = lax.rsqrt(jnp.mean(x * x, axis=-1, keepdims=True) + EPS)
    normed = (x * scale * gain).astype(jnp.bfloat16)
    lane = lax.broadcasted_iota(jnp.int32, (length, pair), 1)
    even = lane < head
    half = head_sum.shape[0]

    def head_scale(part):
        squares = (part * part).astype(jnp.bfloat16)
        sums = jnp.dot(squares, head_sum, preferred_element_type=jnp.float32)
        return part * lax.rsqrt(sums * (1.0 / head) + EPS)

    ones_e = jnp.where(even, 1.0, 0.0).astype(jnp.bfloat16)
    ones_o = jnp.where(even, 0.0, 1.0).astype(jnp.bfloat16)
    zero = jnp.zeros((length, pair), jnp.float32)
    contexts = []
    for start in range(0, width, half):
        wide = slice(start, start + half)
        query = jnp.dot(normed, weight_qkv[:, wide], preferred_element_type=jnp.float32)
        keys = jnp.dot(
            normed,
            weight_qkv[:, width + start : width + start + half],
            preferred_element_type=jnp.float32,
        )
        values = jnp.dot(
            normed,
            weight_qkv[:, 2 * width + start : 2 * width + start + half],
            preferred_element_type=jnp.float32,
        )
        query = (head_scale(query) * (TAU / head)).astype(jnp.bfloat16)
        keys = head_scale(keys)
        for at in range(0, half, pair):
            k = keys[:, at : at + pair]
            v = values[:, at : at + pair]
            k_two = jnp.concatenate(
                [jnp.where(even, k, zero), jnp.where(even, zero, k)], axis=0
            ).astype(jnp.bfloat16)
            scores = lax.dot_general(
                query[:, at : at + pair],
                k_two,
                (((1,), (1,)), ((), ())),
                preferred_element_type=jnp.float32,
            )
            weights = jnp.exp(scores).astype(jnp.bfloat16)
            v_two = jnp.concatenate(
                [
                    jnp.concatenate([jnp.where(even, v, zero).astype(jnp.bfloat16), ones_e], axis=1),
                    jnp.concatenate([jnp.where(even, zero, v).astype(jnp.bfloat16), ones_o], axis=1),
                ],
                axis=0,
            )
            mixed = jnp.dot(weights, v_two, preferred_element_type=jnp.float32)
            contexts.append((mixed[:, :pair] / mixed[:, pair:]).astype(jnp.bfloat16))
    context = jnp.concatenate(contexts, axis=1)
    return x + jnp.dot(context, weight_out[...], preferred_element_type=jnp.float32)


def head_sum_matrix(width):
    head = width // HEADS
    index = jnp.arange(4 * head, dtype=jnp.int32) // head
    return (index[:, None] == index[None, :]).astype(jnp.bfloat16)


def layer_kernel(x_ref, gain_ref, qkv_ref, out_ref, sum_ref, y_ref):
    y_ref[0] = sequence_layer(
        x_ref[0].astype(jnp.float32), gain_ref[...], qkv_ref, out_ref, sum_ref[...]
    ).astype(jnp.bfloat16)


def fused_layer(tokens_in, gain, weight_qkv, weight_out):
    count, length, width = tokens_in.shape
    whole = lambda i: (0, 0)
    block = pl.BlockSpec((1, length, width), lambda i: (i, 0, 0))
    sums = head_sum_matrix(width)
    return pl.pallas_call(
        layer_kernel,
        grid=(count,),
        out_shape=jax.ShapeDtypeStruct(tokens_in.shape, jnp.bfloat16),
        in_specs=[
            block,
            pl.BlockSpec((1, width), whole),
            pl.BlockSpec(weight_qkv.shape, whole),
            pl.BlockSpec(weight_out.shape, whole),
            pl.BlockSpec(sums.shape, whole),
        ],
        out_specs=block,
        compiler_params=pltpu.CompilerParams(vmem_limit_bytes=48 * 1024 * 1024),
        cost_estimate=pl.CostEstimate(
            flops=2 * count * length * width * (4 * width + 2 * length),
            bytes_accessed=4 * count * length * width + 8 * width * width,
            transcendentals=count * HEADS * length * length,
        ),
    )(tokens_in, gain.reshape(1, width), weight_qkv, weight_out, sums)


def fast_body(
    cloud_field,
    row_gain,
    row_qkv,
    row_out,
    col_gain,
    col_qkv,
    col_out,
    plant_cell,
    plant_decoder_device,
    plant_capacity,
    decode_first,
    decode_second,
):
    rows_here, cols_here, width = cloud_field.shape
    strips = lax.axis_size("strip")
    bands = lax.axis_size("band")
    owner_count = bands * strips
    row_share = rows_here // strips
    col_share = cols_here // bands
    both = ("band", "strip")
    rows_in = lax.all_to_all(
        cloud_field.reshape(strips, row_share, cols_here, width),
        "strip",
        split_axis=0,
        concat_axis=2,
        tiled=True,
    )[0]
    mixed_rows = fused_layer(rows_in, row_gain, row_qkv, row_out)
    turned = lax.all_to_all(
        mixed_rows.reshape(row_share, strips, bands, col_share, width)
        .transpose(2, 1, 3, 0, 4)
        .reshape(owner_count, col_share, row_share, width),
        both,
        split_axis=0,
        concat_axis=0,
        tiled=True,
    )
    turned = turned.transpose(1, 0, 2, 3).reshape(col_share, bands * rows_here, width)
    mixed_cols = fused_layer(turned, col_gain, col_qkv, col_out)
    columns_done = mixed_cols.transpose(1, 0, 2)[:, None]
    final_field = lax.all_to_all(
        columns_done, "band", split_axis=0, concat_axis=1, tiled=True
    ).reshape(rows_here, cols_here, width)

    plants_here = plant_cell.shape[0]
    most_slots = 2 * plants_here // owner_count
    features = final_field.reshape(rows_here * cols_here, width)[plant_cell]
    owners = plant_decoder_device[:, 0]
    one_hot = owners[:, None] == jnp.arange(owner_count, dtype=jnp.int32)[None, :]
    counts = one_hot.astype(jnp.int32)
    slot_of = jnp.sum(counts * (jnp.cumsum(counts, axis=0) - 1), axis=1)
    destination = owners * most_slots + slot_of
    place = (
        destination[None, :]
        == jnp.arange(owner_count * most_slots, dtype=jnp.int32)[:, None]
    )
    extra = jnp.zeros((plants_here, 128), jnp.bfloat16)
    extra = extra.at[:, 0].set((plant_capacity // 128).astype(jnp.bfloat16))
    extra = extra.at[:, 1].set((plant_capacity % 128).astype(jnp.bfloat16))
    rows_out = jnp.concatenate([features, extra], axis=1)
    send = jnp.dot(
        place.astype(jnp.bfloat16), rows_out, preferred_element_type=jnp.float32
    ).astype(jnp.bfloat16)
    arrived = lax.all_to_all(send, both, split_axis=0, concat_axis=0, tiled=True)
    hidden = jax.nn.gelu(
        jnp.dot(arrived[:, :width], decode_first, preferred_element_type=jnp.float32)
    ).astype(jnp.bfloat16)
    logit = jnp.sum(
        hidden.astype(jnp.float32) * decode_second[0].astype(jnp.float32)[None, :], axis=1
    )
    yields = jax.nn.softplus(logit)
    capacity = (
        arrived[:, width].astype(jnp.float32) * 128.0 + arrived[:, width + 1].astype(jnp.float32)
    ) * 0.001
    power_here = jnp.sum(capacity * yields)
    back = jnp.concatenate(
        [
            yields.reshape(owner_count, most_slots),
            jnp.broadcast_to(power_here, (owner_count, 1)),
        ],
        axis=1,
    )
    returned = lax.all_to_all(back, both, split_axis=0, concat_axis=0, tiled=True)
    flat = returned[:, :most_slots].reshape(1, owner_count * most_slots)
    own_yield = jnp.sum(jnp.where(place.T, flat, 0.0), axis=1)
    plant_power = plant_capacity.astype(jnp.float32) * 0.001 * own_yield
    fleet_yield = jnp.sum(returned[:, most_slots]) / float(plants_here * owner_count)
    return (final_field, plant_power, fleet_yield)


def body(
    cloud_field,
    row_gain,
    row_qkv,
    row_out,
    col_gain,
    col_qkv,
    col_out,
    plant_cell,
    plant_decoder_device,
    plant_capacity,
    decode_first,
    decode_second,
):
    rows_here, cols_here, model_width = cloud_field.shape
    strips = lax.axis_size("strip")
    bands = lax.axis_size("band")
    owner_count = bands * strips
    row_share = rows_here // strips
    col_share = cols_here // bands
    shape_send = (strips, row_share, cols_here, model_width)
    mixed_rows = mix_layer(
        lax.all_to_all(
            cloud_field.reshape(shape_send), "strip", split_axis=0, concat_axis=2, tiled=True
        )[0],
        row_gain,
        row_qkv,
        row_out,
    )[None]
    after_rows = lax.all_to_all(
        mixed_rows, "strip", split_axis=2, concat_axis=0, tiled=True
    ).reshape(rows_here, cols_here, model_width)
    turned = lax.all_to_all(
        after_rows.reshape(rows_here, bands, col_share, model_width),
        "band",
        split_axis=1,
        concat_axis=0,
        tiled=True,
    )[:, 0].transpose(1, 0, 2)
    mixed_cols = mix_layer(turned, col_gain, col_qkv, col_out)
    columns_done = mixed_cols.transpose(1, 0, 2)[:, None]
    final_field = lax.all_to_all(
        columns_done, "band", split_axis=0, concat_axis=1, tiled=True
    ).reshape(rows_here, cols_here, model_width)
    plants_here = plant_cell.shape[0]
    most_slots = 2 * plants_here // owner_count
    flat_field = final_field.reshape(rows_here * cols_here, model_width)
    features = flat_field[plant_cell]
    owners = plant_decoder_device[:, 0]
    one_hot = (owners[:, None] == jnp.arange(owner_count, dtype=jnp.int32)[None, :]).astype(
        jnp.int32
    )
    running = jnp.cumsum(one_hot, axis=0)
    slot_of = jnp.sum(one_hot * (running - 1), axis=1)
    destination = owners * most_slots + slot_of
    send_buffer = (
        jnp.zeros((owner_count * most_slots, model_width), jnp.bfloat16)
        .at[destination]
        .set(features)
    )
    send_buffer = send_buffer.reshape(owner_count, most_slots, model_width)
    hidden = jax.nn.gelu(
        jnp.einsum(
            "smd,dh->smh",
            lax.all_to_all(send_buffer, ("band", "strip"), split_axis=0, concat_axis=0, tiled=True),
            decode_first,
            preferred_element_type=jnp.float32,
        )
    ).astype(jnp.bfloat16)
    output_logit = jnp.einsum(
        "smh,h->sm", hidden, decode_second[0], preferred_element_type=jnp.float32
    )
    yields = jax.nn.softplus(output_logit)
    returned = lax.all_to_all(yields, ("band", "strip"), split_axis=0, concat_axis=0, tiled=True)
    own_yield = returned.reshape(-1)[destination]
    capacity_w = plant_capacity.astype(jnp.float32) * 0.001
    plant_power = capacity_w * own_yield
    power_sum = lax.psum(jnp.sum(plant_power), ("band", "strip"))
    fleet_yield = power_sum / float(plants_here * owner_count)
    return (final_field, plant_power, fleet_yield)


def solution(mesh):
    grid_fits = 32 * mesh.shape["strip"] == 256 and 64 * mesh.shape["band"] == 256
    return jax.shard_map(
        fast_body if grid_fits else body,
        mesh=mesh,
        in_specs=(
            P("band", "strip", None),
            P(),
            P(),
            P(),
            P(),
            P(),
            P(),
            P(("band", "strip")),
            P(("band", "strip"), None),
            P(("band", "strip")),
            P(("band", "strip"), None),
            P(("band", "strip"), None),
        ),
        out_specs=(P("band", "strip", None), P(("band", "strip")), P()),
        check_vma=False,
    )
```

```python
import jax
import jax.numpy as jnp
from jax import lax
from jax.experimental import pallas as pl
from jax.experimental.pallas import tpu as pltpu
from jax.sharding import PartitionSpec as P

HEADS = 8


EPS = 1e-06
TAU = 12.0


def norm_rows(values, scale_factor):
    widened = values.astype(jnp.float32)
    return (
        widened
        * lax.rsqrt(jnp.mean(widened * widened, axis=-1, keepdims=True) + EPS)
        * scale_factor
    )


def heads_norm(values):
    leading = values.shape[:-1]
    split_up = values.reshape(leading + (HEADS, values.shape[-1] // HEADS))
    normed = split_up * lax.rsqrt(jnp.mean(split_up * split_up, axis=-1, keepdims=True) + EPS)
    return normed.reshape(values.shape)


def project(tokens_in, scale_factor, weight_qkv):
    leading = tokens_in.shape[:-1]
    model_width = tokens_in.shape[-1]
    head_width = model_width // HEADS
    normed = norm_rows(tokens_in, scale_factor).astype(jnp.bfloat16).reshape(-1, model_width)
    projected = jnp.dot(normed, weight_qkv, preferred_element_type=jnp.float32)
    query = heads_norm(projected[:, :model_width]) * (TAU / head_width)
    keys_part = heads_norm(projected[:, model_width : 2 * model_width])
    values_part = projected[:, 2 * model_width :]
    shaped = leading + (model_width,)
    return (
        query.astype(jnp.bfloat16).reshape(shaped),
        keys_part.astype(jnp.bfloat16).reshape(shaped),
        values_part.astype(jnp.bfloat16).reshape(shaped),
    )


def attend(query, keys_part, values_part):
    batch_size, length, model_width = query.shape
    head_width = model_width // HEADS

    def split_heads(tensor):
        return tensor.reshape(batch_size, length, HEADS, head_width).transpose(2, 0, 1, 3)

    def one_head(operands):
        query_rows, key_rows, value_rows = operands
        attention_scores = jnp.einsum(
            "zxe,zle->zxl", query_rows, key_rows, preferred_element_type=jnp.float32
        )
        weights = jnp.exp(attention_scores)
        row_total = jnp.sum(weights, axis=-1, keepdims=True)
        weights_bfloat = (weights / row_total).astype(jnp.bfloat16)
        return jnp.einsum(
            "pem,pmj->pej", weights_bfloat, value_rows, preferred_element_type=jnp.float32
        ).astype(jnp.bfloat16)

    context = lax.map(
        one_head, (split_heads(query), split_heads(keys_part), split_heads(values_part))
    )
    return context.transpose(1, 2, 0, 3).reshape(batch_size, length, model_width)


def finish(tokens_in, context, weight_out):
    model_width = tokens_in.shape[-1]
    mixed = jnp.dot(
        context.reshape(-1, model_width), weight_out, preferred_element_type=jnp.float32
    )
    return (tokens_in.astype(jnp.float32) + mixed.reshape(tokens_in.shape)).astype(jnp.bfloat16)


def mix_layer(tokens_in, scale_factor, weight_qkv, weight_out):
    query, keys_part, values_part = project(tokens_in, scale_factor, weight_qkv)
    return finish(tokens_in, attend(query, keys_part, values_part), weight_out)


def sequence_layer(x, gain, weight_qkv, weight_out, head_sum):
    length, width = x.shape
    head = width // HEADS
    pair = 2 * head
    scale = lax.rsqrt(jnp.mean(x * x, axis=-1, keepdims=True) + EPS)
    normed = (x * scale * gain).astype(jnp.bfloat16)
    lane = lax.broadcasted_iota(jnp.int32, (length, pair), 1)
    even = lane < head
    half = head_sum.shape[0]

    def head_scale(part):
        squares = (part * part).astype(jnp.bfloat16)
        sums = jnp.dot(squares, head_sum, preferred_element_type=jnp.float32)
        return part * lax.rsqrt(sums * (1.0 / head) + EPS)

    ones_e = jnp.where(even, 1.0, 0.0).astype(jnp.bfloat16)
    ones_o = jnp.where(even, 0.0, 1.0).astype(jnp.bfloat16)
    zero = jnp.zeros((length, pair), jnp.float32)
    contexts = []
    for start in range(0, width, half):
        wide = slice(start, start + half)
        query = jnp.dot(normed, weight_qkv[:, wide], preferred_element_type=jnp.float32)
        keys = jnp.dot(
            normed,
            weight_qkv[:, width + start : width + start + half],
            preferred_element_type=jnp.float32,
        )
        values = jnp.dot(
            normed,
            weight_qkv[:, 2 * width + start : 2 * width + start + half],
            preferred_element_type=jnp.float32,
        )
        query = (head_scale(query) * (TAU / head)).astype(jnp.bfloat16)
        keys = head_scale(keys)
        for at in range(0, half, pair):
            k = keys[:, at : at + pair]
            v = values[:, at : at + pair]
            k_two = jnp.concatenate(
                [jnp.where(even, k, zero), jnp.where(even, zero, k)], axis=0
            ).astype(jnp.bfloat16)
            scores = lax.dot_general(
                query[:, at : at + pair],
                k_two,
                (((1,), (1,)), ((), ())),
                preferred_element_type=jnp.float32,
            )
            weights = jnp.exp(scores).astype(jnp.bfloat16)
            v_two = jnp.concatenate(
                [
                    jnp.concatenate([jnp.where(even, v, zero).astype(jnp.bfloat16), ones_e], axis=1),
                    jnp.concatenate([jnp.where(even, zero, v).astype(jnp.bfloat16), ones_o], axis=1),
                ],
                axis=0,
            )
            mixed = jnp.dot(weights, v_two, preferred_element_type=jnp.float32)
            contexts.append((mixed[:, :pair] / mixed[:, pair:]).astype(jnp.bfloat16))
    context = jnp.concatenate(contexts, axis=1)
    return x + jnp.dot(context, weight_out[...], preferred_element_type=jnp.float32)


def head_sum_matrix(width):
    head = width // HEADS
    index = jnp.arange(4 * head, dtype=jnp.int32) // head
    return (index[:, None] == index[None, :]).astype(jnp.bfloat16)


MESH = pl.DeviceIdType.MESH

def whole_kernel(
    cloud, row_gain, row_qkv, row_out, col_gain, col_qkv, col_out, head_sum,
    cells, place, capacity, first, second,
    final, returned,
    rows_in, mixed, rows_out, cols_in, columns, cols_out, blocks_in, field,
    sites_out, sites_in, yields_out,
    rows_sent, rows_got, turn_sent, turn_got, cols_sent, cols_got, site_sems,
):
    strips = lax.axis_size("strip")
    bands = lax.axis_size("band")
    devices = strips * bands
    strip = lax.axis_index("strip")
    band = lax.axis_index("band")
    me = band * strips + strip
    width = cloud.shape[2]
    length = columns.shape[0] // 4

    def wait_bytes(ref, sem):
        pltpu.make_async_copy(ref, ref, sem).wait()

    def split(number):
        return (number // strips, number % strips)

    barrier = pltpu.get_barrier_semaphore()

    @pl.loop(1, devices)
    def _(step):
        pl.semaphore_signal(
            barrier, inc=1, device_id=split((me + step) % devices), device_id_type=MESH
        )

    pl.semaphore_wait(barrier, devices - 1)

    @pl.loop(0, 2)
    def _(part):
        @pl.loop(1, strips)
        def _(step):
            to = (strip + step) % strips
            pltpu.make_async_remote_copy(
                src_ref=cloud.at[pl.ds(to * 8 + part * 4, 4)],
                dst_ref=rows_in.at[part, strip],
                send_sem=rows_sent.at[part],
                recv_sem=rows_got.at[part],
                device_id=(band, to),
                device_id_type=MESH,
            ).start()

        pltpu.make_async_copy(
            cloud.at[pl.ds(strip * 8 + part * 4, 4)], rows_in.at[part, strip], rows_got.at[part]
        ).start()

    @pl.loop(0, 2)
    def _(part):
        wait_bytes(rows_in.at[part], rows_got.at[part])

        @pl.loop(0, 4)
        def _(row):
            x = rows_in[part, :, row].astype(jnp.float32).reshape(length, width)
            y = sequence_layer(x, row_gain[...], row_qkv, row_out, head_sum[...])
            for lanes in range(0, width, 128):
                mixed[lanes // 128, :, pl.ds(pl.multiple_of(row * 8, 8), 8), :] = y[
                    :, lanes : lanes + 128
                ].reshape(devices, 8, 128)

        for parity in range(2):
            for lanes in range(0, width, 128):
                taken = mixed.at[lanes // 128].reshape(devices * 32, 128)[
                    pl.ds(parity, devices * 16, stride=2), :
                ]
                rows_out[part, parity, :, :, lanes : lanes + 128] = (
                    taken.astype(jnp.bfloat16).reshape(devices, 16, 128)
                )

            @pl.loop(1, devices)
            def _(step):
                to_band, to_strip = split((me + step) % devices)
                pltpu.make_async_remote_copy(
                    src_ref=rows_out.at[part, parity, to_strip * bands + to_band],
                    dst_ref=cols_in.at[parity, part, me],
                    send_sem=turn_sent.at[parity, part],
                    recv_sem=turn_got.at[parity, part],
                    device_id=(to_band, to_strip),
                    device_id_type=MESH,
                ).start()

            pltpu.make_async_copy(
                rows_out.at[part, parity, strip * bands + band],
                cols_in.at[parity, part, me],
                turn_got.at[parity, part],
            ).start()

    @pl.loop(0, 2)
    def _(parity):
        for part in range(2):
            wait_bytes(cols_in.at[parity, part], turn_got.at[parity, part])

            @pl.loop(0, devices)
            def _(src):
                at = pl.multiple_of(src * 32 + part * 16, 16)
                for lanes in range(0, width, 128):
                    columns[pl.ds(at, 16), lanes // 128, :] = cols_in[
                        parity, part, src, :, lanes : lanes + 128
                    ].astype(jnp.float32)

        @pl.loop(0, 4)
        def _(number):
            x = jnp.concatenate(
                [
                    columns[pl.ds(number, length, stride=4), lanes, :]
                    for lanes in range(width // 128)
                ],
                axis=1,
            )
            y = sequence_layer(x, col_gain[...], col_qkv, col_out, head_sum[...])
            col = parity * 4 + number
            cols_out[col] = y.astype(jnp.bfloat16).reshape(bands, length // bands, width)

            @pl.loop(1, bands)
            def _(step):
                to = (band + step) % bands
                pltpu.make_async_remote_copy(
                    src_ref=cols_out.at[col, to],
                    dst_ref=blocks_in.at[col, band],
                    send_sem=cols_sent.at[col],
                    recv_sem=cols_got.at[col],
                    device_id=(to, strip),
                    device_id_type=MESH,
                ).start()

            pltpu.make_async_copy(
                cols_out.at[col, band], blocks_in.at[col, band], cols_got.at[col]
            ).start()

    rows_here = cloud.shape[0]
    cols_here = cloud.shape[1]

    @pl.loop(0, 8)
    def _(col):
        wait_bytes(blocks_in.at[col], cols_got.at[col])
        for src in range(4):
            at = src * 8 + 2 * (col % 4) + col // 4
            for lanes in range(0, width, 128):
                field[lanes // 128, pl.ds(at, rows_here, stride=cols_here), :] = blocks_in[
                    col, src, :, lanes : lanes + 128
                ].astype(jnp.float32)

    @pl.loop(0, rows_here // 8)
    def _(row):
        tokens = pl.ds(pl.multiple_of(row * 8 * cols_here, 256), 8 * cols_here)
        for lanes in range(0, width, 128):
            final[pl.ds(row * 8, 8), :, lanes : lanes + 128] = (
                field[lanes // 128, tokens, :].astype(jnp.bfloat16).reshape(8, cols_here, 128)
            )

    tokens = rows_here * cols_here
    at_cell = (
        cells[...] == lax.broadcasted_iota(jnp.int32, (cells.shape[0], tokens), 1)
    ).astype(jnp.bfloat16)
    for lanes in range(0, width, 128):
        features = jnp.dot(
            at_cell, field[lanes // 128].astype(jnp.bfloat16), preferred_element_type=jnp.float32
        ).astype(jnp.bfloat16)
        slots = jnp.dot(place[...], features, preferred_element_type=jnp.float32)
        if lanes == 0:
            slots = slots + capacity[...]
        sites_out[:, :, lanes : lanes + 128] = slots.astype(jnp.bfloat16).reshape(devices, 16, 128)

    @pl.loop(1, devices)
    def _(step):
        to = (me + step) % devices
        pltpu.make_async_remote_copy(
            src_ref=sites_out.at[to],
            dst_ref=sites_in.at[me],
            send_sem=site_sems.at[0],
            recv_sem=site_sems.at[1],
            device_id=split(to),
            device_id_type=MESH,
        ).start()

    pltpu.make_async_copy(sites_out.at[me], sites_in.at[me], site_sems.at[1]).start()
    wait_bytes(sites_in, site_sems.at[1])

    arrived = sites_in[...].reshape(devices * 16, width)
    hidden = jax.nn.gelu(
        jnp.dot(arrived, first[...], preferred_element_type=jnp.float32)
    ).astype(jnp.bfloat16)
    logit = jnp.sum(
        hidden.astype(jnp.float32) * second[...].astype(jnp.float32), axis=1, keepdims=True
    )
    powers = jnp.maximum(logit, 0.0) + jnp.log1p(jnp.exp(-jnp.abs(logit)))
    powers = jnp.broadcast_to(powers, (devices * 16, 128)).reshape(devices, 16, 128)[:, :8]
    lane = lax.broadcasted_iota(jnp.int32, (devices, 8, 128), 2)
    digits = sites_in[:, :, :128].astype(jnp.float32)[:, 8:]
    weight = jnp.where(lane == 0, 0.128, jnp.where(lane == 1, 0.001, 0.0))
    total = jnp.sum(jnp.sum(digits * weight * powers, axis=2, keepdims=True), axis=(0, 1))
    yields_out[...] = jnp.where(lane < 64, powers, total[None, None, :])

    @pl.loop(1, devices)
    def _(step):
        to = (me + step) % devices
        pltpu.make_async_remote_copy(
            src_ref=yields_out.at[to],
            dst_ref=returned.at[me],
            send_sem=site_sems.at[2],
            recv_sem=site_sems.at[3],
            device_id=split(to),
            device_id_type=MESH,
        ).start()

    pltpu.make_async_copy(yields_out.at[me], returned.at[me], site_sems.at[3]).start()
    wait_bytes(returned, site_sems.at[3])

    for part in range(2):
        wait_bytes(rows_in.at[part, pl.ds(0, strips - 1)], rows_sent.at[part])
        for parity in range(2):
            wait_bytes(
                cols_in.at[parity, part, pl.ds(0, devices - 1)], turn_sent.at[parity, part]
            )
    for col in range(8):
        wait_bytes(cols_out.at[col, pl.ds(0, bands - 1)], cols_sent.at[col])
    wait_bytes(sites_out.at[pl.ds(0, devices - 1)], site_sems.at[0])
    wait_bytes(yields_out.at[pl.ds(0, devices - 1)], site_sems.at[2])


def fast_body(
    cloud_field,
    row_gain,
    row_qkv,
    row_out,
    col_gain,
    col_qkv,
    col_out,
    plant_cell,
    plant_decoder_device,
    plant_capacity,
    decode_first,
    decode_second,
):
    rows_here, cols_here, width = cloud_field.shape
    strips = lax.axis_size("strip")
    bands = lax.axis_size("band")
    devices = bands * strips
    length = cols_here * strips
    plants_here = plant_cell.shape[0]

    owners = plant_decoder_device[:, 0]
    counts = (owners[:, None] == jnp.arange(devices, dtype=jnp.int32)[None, :]).astype(jnp.int32)
    slot_of = jnp.sum(counts * (jnp.cumsum(counts, axis=0) - 1), axis=1)
    row_of = owners * 16 + slot_of
    numbers = jnp.arange(devices * 16, dtype=jnp.int32)[:, None]
    place = numbers == row_of[None, :]
    listed = jnp.sum(
        jnp.where(numbers == row_of[None, :] + 8, plant_capacity[None, :], 0),
        axis=1,
        keepdims=True,
    )
    lane = jnp.arange(128, dtype=jnp.int32)[None, :]
    capacity = jnp.where(
        lane == 0, listed // 128, jnp.where(lane == 1, listed % 128, 0)
    ).astype(jnp.float32)

    vmem = pl.BlockSpec(memory_space=pltpu.VMEM)
    bf16 = jnp.bfloat16
    final_field, returned = pl.pallas_call(
        whole_kernel,
        out_shape=(
            jax.ShapeDtypeStruct(cloud_field.shape, bf16),
            jax.ShapeDtypeStruct((devices, 8, 128), jnp.float32),
        ),
        in_specs=[pl.BlockSpec(memory_space=pl.ANY)] + [vmem] * 12,
        out_specs=(vmem, vmem),
        scratch_shapes=[
            pltpu.VMEM((2, strips, 4, cols_here, width), bf16),
            pltpu.VMEM((width // 128, devices, 32, 128), jnp.float32),
            pltpu.VMEM((2, 2, devices, 16, width), bf16),
            pltpu.VMEM((2, 2, devices, 16, width), bf16),
            pltpu.VMEM((4 * length, width // 128, 128), jnp.float32),
            pltpu.VMEM((8, bands, length // bands, width), bf16),
            pltpu.VMEM((8, bands, length // bands, width), bf16),
            pltpu.VMEM((width // 128, rows_here * cols_here, 128), jnp.float32),
            pltpu.VMEM((devices, 16, width), bf16),
            pltpu.VMEM((devices, 16, width), bf16),
            pltpu.VMEM((devices, 8, 128), jnp.float32),
            pltpu.SemaphoreType.DMA((2,)),
            pltpu.SemaphoreType.DMA((2,)),
            pltpu.SemaphoreType.DMA((2, 2)),
            pltpu.SemaphoreType.DMA((2, 2)),
            pltpu.SemaphoreType.DMA((8,)),
            pltpu.SemaphoreType.DMA((8,)),
            pltpu.SemaphoreType.DMA((4,)),
        ],
        compiler_params=pltpu.CompilerParams(
            collective_id=0, has_side_effects=True, vmem_limit_bytes=56 * 1024 * 1024
        ),
        cost_estimate=pl.CostEstimate(
            flops=4 * rows_here * cols_here * width * (4 * width + 2 * length),
            bytes_accessed=8 * cloud_field.size,
            transcendentals=2 * rows_here * cols_here * HEADS * length,
        ),
    )(
        cloud_field,
        row_gain.reshape(1, width),
        row_qkv,
        row_out,
        col_gain.reshape(1, width),
        col_qkv,
        col_out,
        head_sum_matrix(width),
        plant_cell[:, None],
        place.astype(bf16),
        capacity,
        decode_first,
        decode_second,
    )
    yields = jnp.pad(returned[:, :, 0], ((0, 0), (0, 8))).reshape(devices * 16, 1)
    own_yield = jnp.sum(jnp.where(place, yields, 0.0), axis=0)
    plant_power = plant_capacity.astype(jnp.float32) * 0.001 * own_yield
    fleet_yield = jnp.sum(returned[:, 0, 127]) / float(plants_here * devices)
    return (final_field, plant_power, fleet_yield)


def body(
    cloud_field,
    row_gain,
    row_qkv,
    row_out,
    col_gain,
    col_qkv,
    col_out,
    plant_cell,
    plant_decoder_device,
    plant_capacity,
    decode_first,
    decode_second,
):
    rows_here, cols_here, model_width = cloud_field.shape
    strips = lax.axis_size("strip")
    bands = lax.axis_size("band")
    owner_count = bands * strips
    row_share = rows_here // strips
    col_share = cols_here // bands
    shape_send = (strips, row_share, cols_here, model_width)
    mixed_rows = mix_layer(
        lax.all_to_all(
            cloud_field.reshape(shape_send), "strip", split_axis=0, concat_axis=2, tiled=True
        )[0],
        row_gain,
        row_qkv,
        row_out,
    )[None]
    after_rows = lax.all_to_all(
        mixed_rows, "strip", split_axis=2, concat_axis=0, tiled=True
    ).reshape(rows_here, cols_here, model_width)
    turned = lax.all_to_all(
        after_rows.reshape(rows_here, bands, col_share, model_width),
        "band",
        split_axis=1,
        concat_axis=0,
        tiled=True,
    )[:, 0].transpose(1, 0, 2)
    mixed_cols = mix_layer(turned, col_gain, col_qkv, col_out)
    columns_done = mixed_cols.transpose(1, 0, 2)[:, None]
    final_field = lax.all_to_all(
        columns_done, "band", split_axis=0, concat_axis=1, tiled=True
    ).reshape(rows_here, cols_here, model_width)
    plants_here = plant_cell.shape[0]
    most_slots = 2 * plants_here // owner_count
    flat_field = final_field.reshape(rows_here * cols_here, model_width)
    features = flat_field[plant_cell]
    owners = plant_decoder_device[:, 0]
    one_hot = (owners[:, None] == jnp.arange(owner_count, dtype=jnp.int32)[None, :]).astype(
        jnp.int32
    )
    running = jnp.cumsum(one_hot, axis=0)
    slot_of = jnp.sum(one_hot * (running - 1), axis=1)
    destination = owners * most_slots + slot_of
    send_buffer = (
        jnp.zeros((owner_count * most_slots, model_width), jnp.bfloat16)
        .at[destination]
        .set(features)
    )
    send_buffer = send_buffer.reshape(owner_count, most_slots, model_width)
    hidden = jax.nn.gelu(
        jnp.einsum(
            "smd,dh->smh",
            lax.all_to_all(send_buffer, ("band", "strip"), split_axis=0, concat_axis=0, tiled=True),
            decode_first,
            preferred_element_type=jnp.float32,
        )
    ).astype(jnp.bfloat16)
    output_logit = jnp.einsum(
        "smh,h->sm", hidden, decode_second[0], preferred_element_type=jnp.float32
    )
    yields = jax.nn.softplus(output_logit)
    returned = lax.all_to_all(yields, ("band", "strip"), split_axis=0, concat_axis=0, tiled=True)
    own_yield = returned.reshape(-1)[destination]
    capacity_w = plant_capacity.astype(jnp.float32) * 0.001
    plant_power = capacity_w * own_yield
    power_sum = lax.psum(jnp.sum(plant_power), ("band", "strip"))
    fleet_yield = power_sum / float(plants_here * owner_count)
    return (final_field, plant_power, fleet_yield)


def solution(mesh):
    grid_fits = 32 * mesh.shape["strip"] == 256 and 64 * mesh.shape["band"] == 256
    return jax.shard_map(
        fast_body if grid_fits else body,
        mesh=mesh,
        in_specs=(
            P("band", "strip", None),
            P(),
            P(),
            P(),
            P(),
            P(),
            P(),
            P(("band", "strip")),
            P(("band", "strip"), None),
            P(("band", "strip")),
            P(("band", "strip"), None),
            P(("band", "strip"), None),
        ),
        out_specs=(P("band", "strip", None), P(("band", "strip")), P()),
        check_vma=False,
    )
```

```python
import jax
import jax.numpy as jnp
from jax import lax
from jax.experimental import pallas as pl
from jax.experimental.pallas import tpu as pltpu
from jax.sharding import PartitionSpec as P

HEADS = 8


EPS = 1e-06
TAU = 12.0


def norm_rows(values, scale_factor):
    widened = values.astype(jnp.float32)
    return (
        widened
        * lax.rsqrt(jnp.mean(widened * widened, axis=-1, keepdims=True) + EPS)
        * scale_factor
    )


def heads_norm(values):
    leading = values.shape[:-1]
    split_up = values.reshape(leading + (HEADS, values.shape[-1] // HEADS))
    normed = split_up * lax.rsqrt(jnp.mean(split_up * split_up, axis=-1, keepdims=True) + EPS)
    return normed.reshape(values.shape)


def project(tokens_in, scale_factor, weight_qkv):
    leading = tokens_in.shape[:-1]
    model_width = tokens_in.shape[-1]
    head_width = model_width // HEADS
    normed = norm_rows(tokens_in, scale_factor).astype(jnp.bfloat16).reshape(-1, model_width)
    projected = jnp.dot(normed, weight_qkv, preferred_element_type=jnp.float32)
    query = heads_norm(projected[:, :model_width]) * (TAU / head_width)
    keys_part = heads_norm(projected[:, model_width : 2 * model_width])
    values_part = projected[:, 2 * model_width :]
    shaped = leading + (model_width,)
    return (
        query.astype(jnp.bfloat16).reshape(shaped),
        keys_part.astype(jnp.bfloat16).reshape(shaped),
        values_part.astype(jnp.bfloat16).reshape(shaped),
    )


def attend(query, keys_part, values_part):
    batch_size, length, model_width = query.shape
    head_width = model_width // HEADS

    def split_heads(tensor):
        return tensor.reshape(batch_size, length, HEADS, head_width).transpose(2, 0, 1, 3)

    def one_head(operands):
        query_rows, key_rows, value_rows = operands
        attention_scores = jnp.einsum(
            "zxe,zle->zxl", query_rows, key_rows, preferred_element_type=jnp.float32
        )
        weights = jnp.exp(attention_scores)
        row_total = jnp.sum(weights, axis=-1, keepdims=True)
        weights_bfloat = (weights / row_total).astype(jnp.bfloat16)
        return jnp.einsum(
            "pem,pmj->pej", weights_bfloat, value_rows, preferred_element_type=jnp.float32
        ).astype(jnp.bfloat16)

    context = lax.map(
        one_head, (split_heads(query), split_heads(keys_part), split_heads(values_part))
    )
    return context.transpose(1, 2, 0, 3).reshape(batch_size, length, model_width)


def finish(tokens_in, context, weight_out):
    model_width = tokens_in.shape[-1]
    mixed = jnp.dot(
        context.reshape(-1, model_width), weight_out, preferred_element_type=jnp.float32
    )
    return (tokens_in.astype(jnp.float32) + mixed.reshape(tokens_in.shape)).astype(jnp.bfloat16)


def mix_layer(tokens_in, scale_factor, weight_qkv, weight_out):
    query, keys_part, values_part = project(tokens_in, scale_factor, weight_qkv)
    return finish(tokens_in, attend(query, keys_part, values_part), weight_out)


def sequence_layer(x, gain, weight_qkv, weight_out, head_sum):
    length, width = x.shape
    head = width // HEADS
    pair = 2 * head
    scale = lax.rsqrt(jnp.mean(x * x, axis=-1, keepdims=True) + EPS)
    normed = (x * scale * gain).astype(jnp.bfloat16)
    lane = lax.broadcasted_iota(jnp.int32, (length, pair), 1)
    even = lane < head
    half = head_sum.shape[0]

    def head_scale(part):
        squares = (part * part).astype(jnp.bfloat16)
        sums = jnp.dot(squares, head_sum, preferred_element_type=jnp.float32)
        return part * lax.rsqrt(sums * (1.0 / head) + EPS)

    ones_e = jnp.where(even, 1.0, 0.0).astype(jnp.bfloat16)
    ones_o = jnp.where(even, 0.0, 1.0).astype(jnp.bfloat16)
    zero = jnp.zeros((length, pair), jnp.float32)
    contexts = []
    for start in range(0, width, half):
        wide = slice(start, start + half)
        query = jnp.dot(normed, weight_qkv[:, wide], preferred_element_type=jnp.float32)
        keys = jnp.dot(
            normed,
            weight_qkv[:, width + start : width + start + half],
            preferred_element_type=jnp.float32,
        )
        values = jnp.dot(
            normed,
            weight_qkv[:, 2 * width + start : 2 * width + start + half],
            preferred_element_type=jnp.float32,
        )
        query = (head_scale(query) * (TAU / head)).astype(jnp.bfloat16)
        keys = head_scale(keys)
        for at in range(0, half, pair):
            k = keys[:, at : at + pair]
            v = values[:, at : at + pair]
            k_two = jnp.concatenate(
                [jnp.where(even, k, zero), jnp.where(even, zero, k)], axis=0
            ).astype(jnp.bfloat16)
            scores = lax.dot_general(
                query[:, at : at + pair],
                k_two,
                (((1,), (1,)), ((), ())),
                preferred_element_type=jnp.float32,
            )
            weights = jnp.exp(scores).astype(jnp.bfloat16)
            v_two = jnp.concatenate(
                [
                    jnp.concatenate([jnp.where(even, v, zero).astype(jnp.bfloat16), ones_e], axis=1),
                    jnp.concatenate([jnp.where(even, zero, v).astype(jnp.bfloat16), ones_o], axis=1),
                ],
                axis=0,
            )
            mixed = jnp.dot(weights, v_two, preferred_element_type=jnp.float32)
            contexts.append((mixed[:, :pair] / mixed[:, pair:]).astype(jnp.bfloat16))
    context = jnp.concatenate(contexts, axis=1)
    return x + jnp.dot(context, weight_out[...], preferred_element_type=jnp.float32)


def head_sum_matrix(width):
    head = width // HEADS
    index = jnp.arange(4 * head, dtype=jnp.int32) // head
    return (index[:, None] == index[None, :]).astype(jnp.bfloat16)


MESH = pl.DeviceIdType.MESH

def whole_kernel(
    cloud, row_gain, row_qkv, row_out, col_gain, col_qkv, col_out, head_sum,
    cells, owners, capacity, first, second,
    final, power, fleet,
    rows_in, mixed, rows_out, cols_in, columns, cols_out, blocks_in, picks,
    sites_out, sites_in, listed_out, listed_in, yields_out, returned,
    rows_sent, rows_got, turn_sent, turn_got, cols_sent, cols_got, site_sems, done_sems,
):
    strips = lax.axis_size("strip")
    bands = lax.axis_size("band")
    devices = strips * bands
    strip = lax.axis_index("strip")
    band = lax.axis_index("band")
    me = band * strips + strip
    width = cloud.shape[2]
    length = columns.shape[0] // 4

    def wait_bytes(ref, sem):
        pltpu.make_async_copy(ref, ref, sem).wait()

    def split(number):
        return (number // strips, number % strips)

    barrier = pltpu.get_barrier_semaphore()

    @pl.loop(1, devices)
    def _(step):
        pl.semaphore_signal(
            barrier, inc=1, device_id=split((me + step) % devices), device_id_type=MESH
        )

    pl.semaphore_wait(barrier, devices - 1)

    @pl.loop(0, 2)
    def _(part):
        @pl.loop(1, strips)
        def _(step):
            to = (strip + step) % strips
            pltpu.make_async_remote_copy(
                src_ref=cloud.at[pl.ds(to * 8 + part * 4, 4)],
                dst_ref=rows_in.at[part, strip],
                send_sem=rows_sent.at[part],
                recv_sem=rows_got.at[part],
                device_id=(band, to),
                device_id_type=MESH,
            ).start()

        pltpu.make_async_copy(
            cloud.at[pl.ds(strip * 8 + part * 4, 4)], rows_in.at[part, strip], rows_got.at[part]
        ).start()

    plants = cells.shape[1]
    slots = 8
    owner_hot = lax.broadcasted_iota(jnp.int32, (devices, plants), 0) == owners[...]
    owner_one = jnp.where(owner_hot, 1.0, 0.0)
    before = (
        lax.broadcasted_iota(jnp.int32, (plants, plants), 0)
        < lax.broadcasted_iota(jnp.int32, (plants, plants), 1)
    )
    earlier = jnp.dot(
        owner_one.astype(jnp.bfloat16),
        jnp.where(before, 1.0, 0.0).astype(jnp.bfloat16),
        preferred_element_type=jnp.float32,
    )
    slot = jnp.sum(owner_one * earlier, axis=0, keepdims=True).astype(jnp.int32)
    spot = owners[...] * slots + slot
    place = jnp.where(
        lax.broadcasted_iota(jnp.int32, (devices * slots, plants), 0) == spot, 1.0, 0.0
    )
    lane = lax.broadcasted_iota(jnp.int32, (devices, slots, 128), 2)
    own_lane = lane == lax.broadcasted_iota(jnp.int32, (devices, slots, 128), 1)

    def to_lanes(column):
        wide = jnp.broadcast_to(column, (devices * slots, 128)).reshape(devices, slots, 128)
        return jnp.sum(jnp.where(own_lane, wide, 0.0), axis=1, keepdims=True)

    kilowatts = capacity[...].astype(jnp.float32)
    listed_out[...] = to_lanes(jnp.sum(place * kilowatts, axis=1, keepdims=True))

    @pl.loop(1, devices)
    def _(step):
        to = (me + step) % devices
        pltpu.make_async_remote_copy(
            src_ref=listed_out.at[to],
            dst_ref=listed_in.at[me],
            send_sem=site_sems.at[4],
            recv_sem=site_sems.at[5],
            device_id=split(to),
            device_id_type=MESH,
        ).start()

    pltpu.make_async_copy(listed_out.at[me], listed_in.at[me], site_sems.at[5]).start()

    rows_here = cloud.shape[0]
    cols_here = cloud.shape[1]
    cell_row = cells[...] // cols_here
    cell_col = cells[...] % cols_here
    in_block = cell_col // 8 * rows_here + cell_row
    block = cell_col % 2 * 4 + cell_col % 8 // 2

    @pl.loop(0, 8)
    def _(col):
        at_cell = jnp.where(
            lax.broadcasted_iota(jnp.int32, (length, plants), 0)
            == jnp.where(block == col, in_block, -1),
            1.0,
            0.0,
        )
        picks[col] = lax.dot_general(
            place.astype(jnp.bfloat16),
            at_cell.astype(jnp.bfloat16),
            (((1,), (1,)), ((), ())),
            preferred_element_type=jnp.float32,
        ).astype(jnp.bfloat16)

    @pl.loop(0, 2)
    def _(part):
        wait_bytes(rows_in.at[part], rows_got.at[part])

        @pl.loop(0, 4)
        def _(row):
            x = rows_in[part, :, row].astype(jnp.float32).reshape(length, width)
            y = sequence_layer(x, row_gain[...], row_qkv, row_out, head_sum[...])
            for lanes in range(0, width, 128):
                mixed[lanes // 128, :, pl.ds(pl.multiple_of(row * 8, 8), 8), :] = y[
                    :, lanes : lanes + 128
                ].reshape(devices, 8, 128)

        for parity in range(2):
            for lanes in range(0, width, 128):
                taken = mixed.at[lanes // 128].reshape(devices * 32, 128)[
                    pl.ds(parity, devices * 16, stride=2), :
                ]
                rows_out[part, parity, :, :, lanes : lanes + 128] = (
                    taken.astype(jnp.bfloat16).reshape(devices, 16, 128)
                )

            @pl.loop(1, devices)
            def _(step):
                to_band, to_strip = split((me + step) % devices)
                pltpu.make_async_remote_copy(
                    src_ref=rows_out.at[part, parity, to_strip * bands + to_band],
                    dst_ref=cols_in.at[parity, part, me],
                    send_sem=turn_sent.at[parity, part],
                    recv_sem=turn_got.at[parity, part],
                    device_id=(to_band, to_strip),
                    device_id_type=MESH,
                ).start()

            pltpu.make_async_copy(
                rows_out.at[part, parity, strip * bands + band],
                cols_in.at[parity, part, me],
                turn_got.at[parity, part],
            ).start()

    @pl.loop(0, 2)
    def _(parity):
        for part in range(2):
            wait_bytes(cols_in.at[parity, part], turn_got.at[parity, part])

            @pl.loop(0, devices)
            def _(src):
                at = pl.multiple_of(src * 32 + part * 16, 16)
                for lanes in range(0, width, 128):
                    columns[pl.ds(at, 16), lanes // 128, :] = cols_in[
                        parity, part, src, :, lanes : lanes + 128
                    ].astype(jnp.float32)

        @pl.loop(0, 4)
        def _(number):
            x = jnp.concatenate(
                [
                    columns[pl.ds(number, length, stride=4), lanes, :]
                    for lanes in range(width // 128)
                ],
                axis=1,
            )
            y = sequence_layer(x, col_gain[...], col_qkv, col_out, head_sum[...])
            col = parity * 4 + number
            cols_out[col] = y.astype(jnp.bfloat16).reshape(bands, length // bands, width)

            @pl.loop(1, bands)
            def _(step):
                to = (band + step) % bands
                pltpu.make_async_remote_copy(
                    src_ref=cols_out.at[col, to],
                    dst_ref=blocks_in.at[col, band],
                    send_sem=cols_sent.at[col],
                    recv_sem=cols_got.at[col],
                    device_id=(to, strip),
                    device_id_type=MESH,
                ).start()

            pltpu.make_async_copy(
                cols_out.at[col, band], blocks_in.at[col, band], cols_got.at[col]
            ).start()

    sites = jnp.zeros((devices * slots, width), jnp.float32)
    for col in range(8):
        wait_bytes(blocks_in.at[col], cols_got.at[col])
        pltpu.make_async_copy(blocks_in.at[col], final.at[col], done_sems.at[col]).start()
        sites = sites + jnp.dot(
            picks[col],
            blocks_in[col].reshape(length, width),
            preferred_element_type=jnp.float32,
        )
    sites = sites.reshape(devices, slots, width)
    half = width // 2
    sites_out[...] = jnp.concatenate([sites[:, :, :half], sites[:, :, half:]], axis=1).astype(
        jnp.bfloat16
    )

    @pl.loop(1, devices)
    def _(step):
        to = (me + step) % devices
        pltpu.make_async_remote_copy(
            src_ref=sites_out.at[to],
            dst_ref=sites_in.at[me],
            send_sem=site_sems.at[0],
            recv_sem=site_sems.at[1],
            device_id=split(to),
            device_id_type=MESH,
        ).start()

    pltpu.make_async_copy(sites_out.at[me], sites_in.at[me], site_sems.at[1]).start()
    wait_bytes(listed_in, site_sems.at[5])
    wait_bytes(sites_in, site_sems.at[1])

    arrived = sites_in[...].astype(jnp.float32)
    hidden = jnp.dot(
        arrived[:, :slots].reshape(devices * slots, half).astype(jnp.bfloat16),
        first[:half, :],
        preferred_element_type=jnp.float32,
    ) + jnp.dot(
        arrived[:, slots:].reshape(devices * slots, half).astype(jnp.bfloat16),
        first[half:, :],
        preferred_element_type=jnp.float32,
    )
    hidden = jax.nn.gelu(hidden).astype(jnp.bfloat16).astype(jnp.float32)
    logit = jnp.sum(hidden * second[...].astype(jnp.float32), axis=1, keepdims=True)
    yields = to_lanes(jnp.maximum(logit, 0.0) + jnp.log1p(jnp.exp(-jnp.abs(logit))))
    total = jnp.sum(yields * listed_in[...] * 0.001, axis=(0, 2), keepdims=True)
    yields_out[...] = jnp.where(lane[:, :1] == slots, total, yields)

    @pl.loop(1, devices)
    def _(step):
        to = (me + step) % devices
        pltpu.make_async_remote_copy(
            src_ref=yields_out.at[to],
            dst_ref=returned.at[me],
            send_sem=site_sems.at[2],
            recv_sem=site_sems.at[3],
            device_id=split(to),
            device_id_type=MESH,
        ).start()

    pltpu.make_async_copy(yields_out.at[me], returned.at[me], site_sems.at[3]).start()

    for part in range(2):
        wait_bytes(rows_in.at[part, pl.ds(0, strips - 1)], rows_sent.at[part])
        for parity in range(2):
            wait_bytes(
                cols_in.at[parity, part, pl.ds(0, devices - 1)], turn_sent.at[parity, part]
            )
    for col in range(8):
        wait_bytes(cols_out.at[col, pl.ds(0, bands - 1)], cols_sent.at[col])
        wait_bytes(blocks_in.at[col], done_sems.at[col])
    wait_bytes(sites_out.at[pl.ds(0, devices - 1)], site_sems.at[0])
    wait_bytes(listed_out.at[pl.ds(0, devices - 1)], site_sems.at[4])

    wait_bytes(returned, site_sems.at[3])
    back = returned[...].reshape(devices, 128)
    by_slot = lax.dot_general(
        back,
        owner_one,
        (((0,), (0,)), ((), ())),
        precision=lax.Precision.HIGHEST,
        preferred_element_type=jnp.float32,
    )
    own = lax.broadcasted_iota(jnp.int32, (128, plants), 0) == slot
    power[...] = kilowatts * 0.001 * jnp.sum(jnp.where(own, by_slot, 0.0), axis=0, keepdims=True)
    sums = jnp.sum(jnp.where(lane[:, 0] == slots, back, 0.0), axis=(0, 1), keepdims=True)
    fleet[...] = jnp.broadcast_to(sums / float(plants * devices), fleet.shape)
    wait_bytes(yields_out.at[pl.ds(0, devices - 1)], site_sems.at[2])


def fast_body(
    cloud_field,
    row_gain,
    row_qkv,
    row_out,
    col_gain,
    col_qkv,
    col_out,
    plant_cell,
    plant_decoder_device,
    plant_capacity,
    decode_first,
    decode_second,
):
    rows_here, cols_here, width = cloud_field.shape
    strips = lax.axis_size("strip")
    bands = lax.axis_size("band")
    devices = bands * strips
    length = cols_here * strips
    plants_here = plant_cell.shape[0]

    vmem = pl.BlockSpec(memory_space=pltpu.VMEM)
    bf16 = jnp.bfloat16
    final, power, fleet = pl.pallas_call(
        whole_kernel,
        out_shape=(
            jax.ShapeDtypeStruct((8, bands, rows_here, width), bf16),
            jax.ShapeDtypeStruct((1, plants_here), jnp.float32),
            jax.ShapeDtypeStruct((1, 128), jnp.float32),
        ),
        in_specs=[pl.BlockSpec(memory_space=pl.ANY)] + [vmem] * 12,
        out_specs=(pl.BlockSpec(memory_space=pl.ANY), vmem, vmem),
        scratch_shapes=[
            pltpu.VMEM((2, strips, 4, cols_here, width), bf16),
            pltpu.VMEM((width // 128, devices, 32, 128), jnp.float32),
            pltpu.VMEM((2, 2, devices, 16, width), bf16),
            pltpu.VMEM((2, 2, devices, 16, width), bf16),
            pltpu.VMEM((4 * length, width // 128, 128), jnp.float32),
            pltpu.VMEM((8, bands, length // bands, width), bf16),
            pltpu.VMEM((8, bands, length // bands, width), bf16),
            pltpu.VMEM((8, devices * 8, length), bf16),
            pltpu.VMEM((devices, 16, width // 2), bf16),
            pltpu.VMEM((devices, 16, width // 2), bf16),
            pltpu.VMEM((devices, 1, 128), jnp.float32),
            pltpu.VMEM((devices, 1, 128), jnp.float32),
            pltpu.VMEM((devices, 1, 128), jnp.float32),
            pltpu.VMEM((devices, 1, 128), jnp.float32),
            pltpu.SemaphoreType.DMA((2,)),
            pltpu.SemaphoreType.DMA((2,)),
            pltpu.SemaphoreType.DMA((2, 2)),
            pltpu.SemaphoreType.DMA((2, 2)),
            pltpu.SemaphoreType.DMA((8,)),
            pltpu.SemaphoreType.DMA((8,)),
            pltpu.SemaphoreType.DMA((6,)),
            pltpu.SemaphoreType.DMA((8,)),
        ],
        compiler_params=pltpu.CompilerParams(
            collective_id=0, has_side_effects=True, vmem_limit_bytes=56 * 1024 * 1024
        ),
        cost_estimate=pl.CostEstimate(
            flops=4 * rows_here * cols_here * width * (4 * width + 2 * length),
            bytes_accessed=8 * cloud_field.size,
            transcendentals=2 * rows_here * cols_here * HEADS * length,
        ),
    )(
        cloud_field,
        row_gain.reshape(1, width),
        row_qkv,
        row_out,
        col_gain.reshape(1, width),
        col_qkv,
        col_out,
        head_sum_matrix(width),
        plant_cell.reshape(1, plants_here),
        plant_decoder_device.reshape(1, plants_here),
        plant_capacity.reshape(1, plants_here),
        decode_first,
        decode_second,
    )
    final_field = (
        final.reshape(2, 4, bands, rows_here, width)
        .transpose(3, 2, 1, 0, 4)
        .reshape(rows_here, cols_here, width)
    )
    return (final_field, power[0], fleet[0, 0])


def body(
    cloud_field,
    row_gain,
    row_qkv,
    row_out,
    col_gain,
    col_qkv,
    col_out,
    plant_cell,
    plant_decoder_device,
    plant_capacity,
    decode_first,
    decode_second,
):
    rows_here, cols_here, model_width = cloud_field.shape
    strips = lax.axis_size("strip")
    bands = lax.axis_size("band")
    owner_count = bands * strips
    row_share = rows_here // strips
    col_share = cols_here // bands
    shape_send = (strips, row_share, cols_here, model_width)
    mixed_rows = mix_layer(
        lax.all_to_all(
            cloud_field.reshape(shape_send), "strip", split_axis=0, concat_axis=2, tiled=True
        )[0],
        row_gain,
        row_qkv,
        row_out,
    )[None]
    after_rows = lax.all_to_all(
        mixed_rows, "strip", split_axis=2, concat_axis=0, tiled=True
    ).reshape(rows_here, cols_here, model_width)
    turned = lax.all_to_all(
        after_rows.reshape(rows_here, bands, col_share, model_width),
        "band",
        split_axis=1,
        concat_axis=0,
        tiled=True,
    )[:, 0].transpose(1, 0, 2)
    mixed_cols = mix_layer(turned, col_gain, col_qkv, col_out)
    columns_done = mixed_cols.transpose(1, 0, 2)[:, None]
    final_field = lax.all_to_all(
        columns_done, "band", split_axis=0, concat_axis=1, tiled=True
    ).reshape(rows_here, cols_here, model_width)
    plants_here = plant_cell.shape[0]
    most_slots = 2 * plants_here // owner_count
    flat_field = final_field.reshape(rows_here * cols_here, model_width)
    features = flat_field[plant_cell]
    owners = plant_decoder_device[:, 0]
    one_hot = (owners[:, None] == jnp.arange(owner_count, dtype=jnp.int32)[None, :]).astype(
        jnp.int32
    )
    running = jnp.cumsum(one_hot, axis=0)
    slot_of = jnp.sum(one_hot * (running - 1), axis=1)
    destination = owners * most_slots + slot_of
    send_buffer = (
        jnp.zeros((owner_count * most_slots, model_width), jnp.bfloat16)
        .at[destination]
        .set(features)
    )
    send_buffer = send_buffer.reshape(owner_count, most_slots, model_width)
    hidden = jax.nn.gelu(
        jnp.einsum(
            "smd,dh->smh",
            lax.all_to_all(send_buffer, ("band", "strip"), split_axis=0, concat_axis=0, tiled=True),
            decode_first,
            preferred_element_type=jnp.float32,
        )
    ).astype(jnp.bfloat16)
    output_logit = jnp.einsum(
        "smh,h->sm", hidden, decode_second[0], preferred_element_type=jnp.float32
    )
    yields = jax.nn.softplus(output_logit)
    returned = lax.all_to_all(yields, ("band", "strip"), split_axis=0, concat_axis=0, tiled=True)
    own_yield = returned.reshape(-1)[destination]
    capacity_w = plant_capacity.astype(jnp.float32) * 0.001
    plant_power = capacity_w * own_yield
    power_sum = lax.psum(jnp.sum(plant_power), ("band", "strip"))
    fleet_yield = power_sum / float(plants_here * owner_count)
    return (final_field, plant_power, fleet_yield)


def solution(mesh):
    grid_fits = 32 * mesh.shape["strip"] == 256 and 64 * mesh.shape["band"] == 256
    return jax.shard_map(
        fast_body if grid_fits else body,
        mesh=mesh,
        in_specs=(
            P("band", "strip", None),
            P(),
            P(),
            P(),
            P(),
            P(),
            P(),
            P(("band", "strip")),
            P(("band", "strip"), None),
            P(("band", "strip")),
            P(("band", "strip"), None),
            P(("band", "strip"), None),
        ),
        out_specs=(P("band", "strip", None), P(("band", "strip")), P()),
        check_vma=False,
    )
```

```python
import jax
import jax.numpy as jnp
from jax import lax
from jax.experimental import pallas as pl
from jax.experimental.pallas import tpu as pltpu
from jax.sharding import PartitionSpec as P

HEADS = 8


EPS = 1e-06
TAU = 12.0
LOG2_E = 1.4426950408889634


def norm_rows(values, scale_factor):
    widened = values.astype(jnp.float32)
    return (
        widened
        * lax.rsqrt(jnp.mean(widened * widened, axis=-1, keepdims=True) + EPS)
        * scale_factor
    )


def heads_norm(values):
    leading = values.shape[:-1]
    split_up = values.reshape(leading + (HEADS, values.shape[-1] // HEADS))
    normed = split_up * lax.rsqrt(jnp.mean(split_up * split_up, axis=-1, keepdims=True) + EPS)
    return normed.reshape(values.shape)


def project(tokens_in, scale_factor, weight_qkv):
    leading = tokens_in.shape[:-1]
    model_width = tokens_in.shape[-1]
    head_width = model_width // HEADS
    normed = norm_rows(tokens_in, scale_factor).astype(jnp.bfloat16).reshape(-1, model_width)
    projected = jnp.dot(normed, weight_qkv, preferred_element_type=jnp.float32)
    query = heads_norm(projected[:, :model_width]) * (TAU / head_width)
    keys_part = heads_norm(projected[:, model_width : 2 * model_width])
    values_part = projected[:, 2 * model_width :]
    shaped = leading + (model_width,)
    return (
        query.astype(jnp.bfloat16).reshape(shaped),
        keys_part.astype(jnp.bfloat16).reshape(shaped),
        values_part.astype(jnp.bfloat16).reshape(shaped),
    )


def attend(query, keys_part, values_part):
    batch_size, length, model_width = query.shape
    head_width = model_width // HEADS

    def split_heads(tensor):
        return tensor.reshape(batch_size, length, HEADS, head_width).transpose(2, 0, 1, 3)

    def one_head(operands):
        query_rows, key_rows, value_rows = operands
        attention_scores = jnp.einsum(
            "zxe,zle->zxl", query_rows, key_rows, preferred_element_type=jnp.float32
        )
        weights = jnp.exp(attention_scores)
        row_total = jnp.sum(weights, axis=-1, keepdims=True)
        weights_bfloat = (weights / row_total).astype(jnp.bfloat16)
        return jnp.einsum(
            "pem,pmj->pej", weights_bfloat, value_rows, preferred_element_type=jnp.float32
        ).astype(jnp.bfloat16)

    context = lax.map(
        one_head, (split_heads(query), split_heads(keys_part), split_heads(values_part))
    )
    return context.transpose(1, 2, 0, 3).reshape(batch_size, length, model_width)


def finish(tokens_in, context, weight_out):
    model_width = tokens_in.shape[-1]
    mixed = jnp.dot(
        context.reshape(-1, model_width), weight_out, preferred_element_type=jnp.float32
    )
    return (tokens_in.astype(jnp.float32) + mixed.reshape(tokens_in.shape)).astype(jnp.bfloat16)


def mix_layer(tokens_in, scale_factor, weight_qkv, weight_out):
    query, keys_part, values_part = project(tokens_in, scale_factor, weight_qkv)
    return finish(tokens_in, attend(query, keys_part, values_part), weight_out)


def sequence_layer(x, gain, weight_qkv, weight_out, head_sum):
    length, width = x.shape
    head = width // HEADS
    pair = 2 * head
    scale = lax.rsqrt(jnp.mean(x * x, axis=-1, keepdims=True) + EPS)
    normed = (x * scale * gain).astype(jnp.bfloat16)
    lane = lax.broadcasted_iota(jnp.int32, (length, pair), 1)
    even = lane < head
    half = head_sum.shape[0]

    def head_scale(part):
        squares = (part * part).astype(jnp.bfloat16)
        sums = jnp.dot(squares, head_sum, preferred_element_type=jnp.float32)
        return part * lax.rsqrt(sums * (1.0 / head) + EPS)

    ones_e = jnp.where(even, 1.0, 0.0).astype(jnp.bfloat16)
    ones_o = jnp.where(even, 0.0, 1.0).astype(jnp.bfloat16)
    zero = jnp.zeros((length, pair), jnp.float32)
    contexts = []
    for start in range(0, width, half):
        wide = slice(start, start + half)
        query = jnp.dot(normed, weight_qkv[:, wide], preferred_element_type=jnp.float32)
        keys = jnp.dot(
            normed,
            weight_qkv[:, width + start : width + start + half],
            preferred_element_type=jnp.float32,
        )
        values = jnp.dot(
            normed,
            weight_qkv[:, 2 * width + start : 2 * width + start + half],
            preferred_element_type=jnp.float32,
        )
        query = (head_scale(query) * (TAU / head * LOG2_E)).astype(jnp.bfloat16)
        keys = head_scale(keys)
        for at in range(0, half, pair):
            k = keys[:, at : at + pair]
            v = values[:, at : at + pair]
            k_two = jnp.concatenate(
                [jnp.where(even, k, zero), jnp.where(even, zero, k)], axis=0
            ).astype(jnp.bfloat16)
            scores = lax.dot_general(
                query[:, at : at + pair],
                k_two,
                (((1,), (1,)), ((), ())),
                preferred_element_type=jnp.float32,
            )
            weights = jnp.exp2(scores).astype(jnp.bfloat16)
            v_two = jnp.concatenate(
                [
                    jnp.concatenate([jnp.where(even, v, zero).astype(jnp.bfloat16), ones_e], axis=1),
                    jnp.concatenate([jnp.where(even, zero, v).astype(jnp.bfloat16), ones_o], axis=1),
                ],
                axis=0,
            )
            mixed = jnp.dot(weights, v_two, preferred_element_type=jnp.float32)
            contexts.append((mixed[:, :pair] / mixed[:, pair:]).astype(jnp.bfloat16))
    context = jnp.concatenate(contexts, axis=1)
    return x + jnp.dot(context, weight_out[...], preferred_element_type=jnp.float32)


def head_sum_matrix(width):
    head = width // HEADS
    index = jnp.arange(4 * head, dtype=jnp.int32) // head
    return (index[:, None] == index[None, :]).astype(jnp.bfloat16)


MESH = pl.DeviceIdType.MESH

def whole_kernel(
    cloud, row_gain, row_qkv, row_out, col_gain, col_qkv, col_out, head_sum,
    cells, owners, capacity, first, second,
    final, power, fleet,
    rows_in, mixed, rows_out, cols_in, columns, cols_out, blocks_in, picks,
    sites_out, sites_in, listed_out, listed_in, yields_out, returned,
    rows_sent, rows_got, turn_sent, turn_got, cols_sent, cols_got, site_sems, done_sems,
):
    strips = lax.axis_size("strip")
    bands = lax.axis_size("band")
    devices = strips * bands
    strip = lax.axis_index("strip")
    band = lax.axis_index("band")
    me = band * strips + strip
    width = cloud.shape[2]
    length = columns.shape[1] // 4

    def wait_bytes(ref, sem):
        pltpu.make_async_copy(ref, ref, sem).wait()

    def split(number):
        return (number // strips, number % strips)

    barrier = pltpu.get_barrier_semaphore()

    @pl.loop(1, devices)
    def _(step):
        pl.semaphore_signal(
            barrier, inc=1, device_id=split((me + step) % devices), device_id_type=MESH
        )

    pl.semaphore_wait(barrier, devices - 1)

    @pl.loop(0, 4)
    def _(part):
        @pl.loop(1, strips)
        def _(step):
            to = (strip + step) % strips
            pltpu.make_async_remote_copy(
                src_ref=cloud.at[pl.ds(to * 8 + part * 2, 2)],
                dst_ref=rows_in.at[part, strip],
                send_sem=rows_sent.at[part],
                recv_sem=rows_got.at[part],
                device_id=(band, to),
                device_id_type=MESH,
            ).start()

        pltpu.make_async_copy(
            cloud.at[pl.ds(strip * 8 + part * 2, 2)], rows_in.at[part, strip], rows_got.at[part]
        ).start()

    plants = cells.shape[1]
    slots = 8
    owner_hot = lax.broadcasted_iota(jnp.int32, (devices, plants), 0) == owners[...]
    owner_one = jnp.where(owner_hot, 1.0, 0.0)
    before = (
        lax.broadcasted_iota(jnp.int32, (plants, plants), 0)
        < lax.broadcasted_iota(jnp.int32, (plants, plants), 1)
    )
    earlier = jnp.dot(
        owner_one.astype(jnp.bfloat16),
        jnp.where(before, 1.0, 0.0).astype(jnp.bfloat16),
        preferred_element_type=jnp.float32,
    )
    slot = jnp.sum(owner_one * earlier, axis=0, keepdims=True).astype(jnp.int32)
    spot = owners[...] * slots + slot
    place = jnp.where(
        lax.broadcasted_iota(jnp.int32, (devices * slots, plants), 0) == spot, 1.0, 0.0
    )
    lane = lax.broadcasted_iota(jnp.int32, (devices, slots, 128), 2)
    own_lane = lane == lax.broadcasted_iota(jnp.int32, (devices, slots, 128), 1)

    def to_lanes(column):
        wide = jnp.broadcast_to(column, (devices * slots, 128)).reshape(devices, slots, 128)
        return jnp.sum(jnp.where(own_lane, wide, 0.0), axis=1, keepdims=True)

    kilowatts = capacity[...].astype(jnp.float32)
    listed_out[...] = to_lanes(jnp.sum(place * kilowatts, axis=1, keepdims=True))

    @pl.loop(1, devices)
    def _(step):
        to = (me + step) % devices
        pltpu.make_async_remote_copy(
            src_ref=listed_out.at[to],
            dst_ref=listed_in.at[me],
            send_sem=site_sems.at[4],
            recv_sem=site_sems.at[5],
            device_id=split(to),
            device_id_type=MESH,
        ).start()

    pltpu.make_async_copy(listed_out.at[me], listed_in.at[me], site_sems.at[5]).start()

    rows_here = cloud.shape[0]
    cols_here = cloud.shape[1]
    cell_row = cells[...] // cols_here
    cell_col = cells[...] % cols_here
    in_block = cell_col // 8 * rows_here + cell_row
    block = cell_col % 2 * 4 + cell_col % 8 // 2

    @pl.loop(0, 8)
    def _(col):
        at_cell = jnp.where(
            lax.broadcasted_iota(jnp.int32, (length, plants), 0)
            == jnp.where(block == col, in_block, -1),
            1.0,
            0.0,
        )
        picks[col] = lax.dot_general(
            place.astype(jnp.bfloat16),
            at_cell.astype(jnp.bfloat16),
            (((1,), (1,)), ((), ())),
            preferred_element_type=jnp.float32,
        ).astype(jnp.bfloat16)

    @pl.loop(0, 2)
    def _(part):
        @pl.loop(0, 4)
        def _(row):
            pair = part * 2 + row // 2

            @pl.when(row % 2 == 0)
            def _():
                wait_bytes(rows_in.at[pair], rows_got.at[pair])

            x = rows_in[pair, :, row % 2].astype(jnp.float32).reshape(length, width)
            y = sequence_layer(x, row_gain[...], row_qkv, row_out, head_sum[...])
            for lanes in range(0, width, 128):
                mixed[lanes // 128, :, pl.ds(pl.multiple_of(row * 8, 8), 8), :] = y[
                    :, lanes : lanes + 128
                ].reshape(devices, 8, 128)

        for parity in range(2):
            for lanes in range(0, width, 128):
                taken = mixed.at[lanes // 128].reshape(devices * 32, 128)[
                    pl.ds(parity, devices * 16, stride=2), :
                ]
                rows_out[part, parity, :, :, lanes : lanes + 128] = (
                    taken.astype(jnp.bfloat16).reshape(devices, 16, 128)
                )

            @pl.loop(1, devices)
            def _(step):
                to_band, to_strip = split((me + step) % devices)
                pltpu.make_async_remote_copy(
                    src_ref=rows_out.at[part, parity, to_strip * bands + to_band],
                    dst_ref=cols_in.at[parity, part, me],
                    send_sem=turn_sent.at[parity, part],
                    recv_sem=turn_got.at[parity, part],
                    device_id=(to_band, to_strip),
                    device_id_type=MESH,
                ).start()

            pltpu.make_async_copy(
                rows_out.at[part, parity, strip * bands + band],
                cols_in.at[parity, part, me],
                turn_got.at[parity, part],
            ).start()

    @pl.loop(0, 2)
    def _(parity):
        for part in range(2):
            wait_bytes(cols_in.at[parity, part], turn_got.at[parity, part])

            @pl.loop(0, devices)
            def _(src):
                at = pl.multiple_of(src * 32 + part * 16, 16)
                for lanes in range(0, width, 128):
                    columns[lanes // 128, pl.ds(at, 16), :] = cols_in[
                        parity, part, src, :, lanes : lanes + 128
                    ].astype(jnp.float32)

        @pl.loop(0, 4)
        def _(number):
            x = jnp.concatenate(
                [
                    columns[lanes, pl.ds(number, length, stride=4), :]
                    for lanes in range(width // 128)
                ],
                axis=1,
            )
            y = sequence_layer(x, col_gain[...], col_qkv, col_out, head_sum[...])
            col = parity * 4 + number
            cols_out[col] = y.astype(jnp.bfloat16).reshape(bands, length // bands, width)

            @pl.loop(1, bands)
            def _(step):
                to = (band + step) % bands
                pltpu.make_async_remote_copy(
                    src_ref=cols_out.at[col, to],
                    dst_ref=blocks_in.at[col, band],
                    send_sem=cols_sent.at[col],
                    recv_sem=cols_got.at[col],
                    device_id=(to, strip),
                    device_id_type=MESH,
                ).start()

            pltpu.make_async_copy(
                cols_out.at[col, band], blocks_in.at[col, band], cols_got.at[col]
            ).start()

    sites = jnp.zeros((devices * slots, width), jnp.float32)
    for col in range(8):
        wait_bytes(blocks_in.at[col], cols_got.at[col])
        pltpu.make_async_copy(blocks_in.at[col], final.at[col], done_sems.at[col]).start()
        sites = sites + jnp.dot(
            picks[col],
            blocks_in[col].reshape(length, width),
            preferred_element_type=jnp.float32,
        )
    sites = sites.reshape(devices, slots, width)
    half = width // 2
    sites_out[...] = jnp.concatenate([sites[:, :, :half], sites[:, :, half:]], axis=1).astype(
        jnp.bfloat16
    )

    @pl.loop(1, devices)
    def _(step):
        to = (me + step) % devices
        pltpu.make_async_remote_copy(
            src_ref=sites_out.at[to],
            dst_ref=sites_in.at[me],
            send_sem=site_sems.at[0],
            recv_sem=site_sems.at[1],
            device_id=split(to),
            device_id_type=MESH,
        ).start()

    pltpu.make_async_copy(sites_out.at[me], sites_in.at[me], site_sems.at[1]).start()
    wait_bytes(listed_in, site_sems.at[5])
    wait_bytes(sites_in, site_sems.at[1])

    arrived = sites_in[...].astype(jnp.float32)
    hidden = jnp.dot(
        arrived[:, :slots].reshape(devices * slots, half).astype(jnp.bfloat16),
        first[:half, :],
        preferred_element_type=jnp.float32,
    ) + jnp.dot(
        arrived[:, slots:].reshape(devices * slots, half).astype(jnp.bfloat16),
        first[half:, :],
        preferred_element_type=jnp.float32,
    )
    hidden = jax.nn.gelu(hidden).astype(jnp.bfloat16).astype(jnp.float32)
    logit = jnp.sum(hidden * second[...].astype(jnp.float32), axis=1, keepdims=True)
    yields = to_lanes(jnp.maximum(logit, 0.0) + jnp.log1p(jnp.exp(-jnp.abs(logit))))
    total = jnp.sum(yields * listed_in[...] * 0.001, axis=(0, 2), keepdims=True)
    yields_out[...] = jnp.where(lane[:, :1] == slots, total, yields)

    @pl.loop(1, devices)
    def _(step):
        to = (me + step) % devices
        pltpu.make_async_remote_copy(
            src_ref=yields_out.at[to],
            dst_ref=returned.at[me],
            send_sem=site_sems.at[2],
            recv_sem=site_sems.at[3],
            device_id=split(to),
            device_id_type=MESH,
        ).start()

    pltpu.make_async_copy(yields_out.at[me], returned.at[me], site_sems.at[3]).start()

    for pair in range(4):
        wait_bytes(rows_in.at[pair, pl.ds(0, strips - 1)], rows_sent.at[pair])
    for part in range(2):
        for parity in range(2):
            wait_bytes(
                cols_in.at[parity, part, pl.ds(0, devices - 1)], turn_sent.at[parity, part]
            )
    for col in range(8):
        wait_bytes(cols_out.at[col, pl.ds(0, bands - 1)], cols_sent.at[col])
        wait_bytes(blocks_in.at[col], done_sems.at[col])
    wait_bytes(sites_out.at[pl.ds(0, devices - 1)], site_sems.at[0])
    wait_bytes(listed_out.at[pl.ds(0, devices - 1)], site_sems.at[4])

    wait_bytes(returned, site_sems.at[3])
    back = returned[...].reshape(devices, 128)
    by_slot = lax.dot_general(
        back,
        owner_one,
        (((0,), (0,)), ((), ())),
        precision=lax.Precision.HIGHEST,
        preferred_element_type=jnp.float32,
    )
    own = lax.broadcasted_iota(jnp.int32, (128, plants), 0) == slot
    power[...] = kilowatts * 0.001 * jnp.sum(jnp.where(own, by_slot, 0.0), axis=0, keepdims=True)
    sums = jnp.sum(jnp.where(lane[:, 0] == slots, back, 0.0), axis=(0, 1), keepdims=True)
    fleet[...] = jnp.broadcast_to(sums / float(plants * devices), fleet.shape)
    wait_bytes(yields_out.at[pl.ds(0, devices - 1)], site_sems.at[2])


def assemble_kernel(blocks, out, tile):
    parts, bands, rows, width = blocks.shape
    cols = parts * bands
    for lanes in range(0, width, 128):
        for part in range(parts):
            for band in range(bands):
                at = band * parts + 2 * (part % 4) + part // 4
                tile[lanes // 128, pl.ds(at, rows, stride=cols), :] = blocks[
                    part, band, :, lanes : lanes + 128
                ].astype(jnp.float32)
        out[:, :, lanes : lanes + 128] = (
            tile[lanes // 128].astype(jnp.bfloat16).reshape(rows, cols, 128)
        )


def assemble(blocks):
    parts, bands, rows, width = blocks.shape
    step = 16
    cols = parts * bands
    return pl.pallas_call(
        assemble_kernel,
        grid=(rows // step,),
        out_shape=jax.ShapeDtypeStruct((rows, cols, width), blocks.dtype),
        in_specs=[pl.BlockSpec((parts, bands, step, width), lambda i: (0, 0, i, 0))],
        out_specs=pl.BlockSpec((step, cols, width), lambda i: (i, 0, 0)),
        scratch_shapes=[pltpu.VMEM((width // 128, step * cols, 128), jnp.float32)],
        compiler_params=pltpu.CompilerParams(vmem_limit_bytes=60 * 1024 * 1024),
        cost_estimate=pl.CostEstimate(
            flops=0, bytes_accessed=4 * blocks.size, transcendentals=0
        ),
    )(blocks)


def fast_body(
    cloud_field,
    row_gain,
    row_qkv,
    row_out,
    col_gain,
    col_qkv,
    col_out,
    plant_cell,
    plant_decoder_device,
    plant_capacity,
    decode_first,
    decode_second,
):
    rows_here, cols_here, width = cloud_field.shape
    strips = lax.axis_size("strip")
    bands = lax.axis_size("band")
    devices = bands * strips
    length = cols_here * strips
    plants_here = plant_cell.shape[0]

    vmem = pl.BlockSpec(memory_space=pltpu.VMEM)
    bf16 = jnp.bfloat16
    final, power, fleet = pl.pallas_call(
        whole_kernel,
        out_shape=(
            jax.ShapeDtypeStruct((8, bands, rows_here, width), bf16),
            jax.ShapeDtypeStruct((1, plants_here), jnp.float32),
            jax.ShapeDtypeStruct((1, 128), jnp.float32),
        ),
        in_specs=[pl.BlockSpec(memory_space=pl.ANY)] + [vmem] * 12,
        out_specs=(pl.BlockSpec(memory_space=pl.ANY), vmem, vmem),
        scratch_shapes=[
            pltpu.VMEM((4, strips, 2, cols_here, width), bf16),
            pltpu.VMEM((width // 128, devices, 32, 128), jnp.float32),
            pltpu.VMEM((2, 2, devices, 16, width), bf16),
            pltpu.VMEM((2, 2, devices, 16, width), bf16),
            pltpu.VMEM((width // 128, 4 * length, 128), jnp.float32),
            pltpu.VMEM((8, bands, length // bands, width), bf16),
            pltpu.VMEM((8, bands, length // bands, width), bf16),
            pltpu.VMEM((8, devices * 8, length), bf16),
            pltpu.VMEM((devices, 16, width // 2), bf16),
            pltpu.VMEM((devices, 16, width // 2), bf16),
            pltpu.VMEM((devices, 1, 128), jnp.float32),
            pltpu.VMEM((devices, 1, 128), jnp.float32),
            pltpu.VMEM((devices, 1, 128), jnp.float32),
            pltpu.VMEM((devices, 1, 128), jnp.float32),
            pltpu.SemaphoreType.DMA((4,)),
            pltpu.SemaphoreType.DMA((4,)),
            pltpu.SemaphoreType.DMA((2, 2)),
            pltpu.SemaphoreType.DMA((2, 2)),
            pltpu.SemaphoreType.DMA((8,)),
            pltpu.SemaphoreType.DMA((8,)),
            pltpu.SemaphoreType.DMA((6,)),
            pltpu.SemaphoreType.DMA((8,)),
        ],
        compiler_params=pltpu.CompilerParams(
            collective_id=0, has_side_effects=True, vmem_limit_bytes=56 * 1024 * 1024
        ),
        cost_estimate=pl.CostEstimate(
            flops=4 * rows_here * cols_here * width * (4 * width + 2 * length),
            bytes_accessed=8 * cloud_field.size,
            transcendentals=2 * rows_here * cols_here * HEADS * length,
        ),
    )(
        cloud_field,
        row_gain.reshape(1, width),
        row_qkv,
        row_out,
        col_gain.reshape(1, width),
        col_qkv,
        col_out,
        head_sum_matrix(width),
        plant_cell.reshape(1, plants_here),
        plant_decoder_device.reshape(1, plants_here),
        plant_capacity.reshape(1, plants_here),
        decode_first,
        decode_second,
    )
    final_field = assemble(final)
    return (final_field, power[0], fleet[0, 0])


def body(
    cloud_field,
    row_gain,
    row_qkv,
    row_out,
    col_gain,
    col_qkv,
    col_out,
    plant_cell,
    plant_decoder_device,
    plant_capacity,
    decode_first,
    decode_second,
):
    rows_here, cols_here, model_width = cloud_field.shape
    strips = lax.axis_size("strip")
    bands = lax.axis_size("band")
    owner_count = bands * strips
    row_share = rows_here // strips
    col_share = cols_here // bands
    shape_send = (strips, row_share, cols_here, model_width)
    mixed_rows = mix_layer(
        lax.all_to_all(
            cloud_field.reshape(shape_send), "strip", split_axis=0, concat_axis=2, tiled=True
        )[0],
        row_gain,
        row_qkv,
        row_out,
    )[None]
    after_rows = lax.all_to_all(
        mixed_rows, "strip", split_axis=2, concat_axis=0, tiled=True
    ).reshape(rows_here, cols_here, model_width)
    turned = lax.all_to_all(
        after_rows.reshape(rows_here, bands, col_share, model_width),
        "band",
        split_axis=1,
        concat_axis=0,
        tiled=True,
    )[:, 0].transpose(1, 0, 2)
    mixed_cols = mix_layer(turned, col_gain, col_qkv, col_out)
    columns_done = mixed_cols.transpose(1, 0, 2)[:, None]
    final_field = lax.all_to_all(
        columns_done, "band", split_axis=0, concat_axis=1, tiled=True
    ).reshape(rows_here, cols_here, model_width)
    plants_here = plant_cell.shape[0]
    most_slots = 2 * plants_here // owner_count
    flat_field = final_field.reshape(rows_here * cols_here, model_width)
    features = flat_field[plant_cell]
    owners = plant_decoder_device[:, 0]
    one_hot = (owners[:, None] == jnp.arange(owner_count, dtype=jnp.int32)[None, :]).astype(
        jnp.int32
    )
    running = jnp.cumsum(one_hot, axis=0)
    slot_of = jnp.sum(one_hot * (running - 1), axis=1)
    destination = owners * most_slots + slot_of
    send_buffer = (
        jnp.zeros((owner_count * most_slots, model_width), jnp.bfloat16)
        .at[destination]
        .set(features)
    )
    send_buffer = send_buffer.reshape(owner_count, most_slots, model_width)
    hidden = jax.nn.gelu(
        jnp.einsum(
            "smd,dh->smh",
            lax.all_to_all(send_buffer, ("band", "strip"), split_axis=0, concat_axis=0, tiled=True),
            decode_first,
            preferred_element_type=jnp.float32,
        )
    ).astype(jnp.bfloat16)
    output_logit = jnp.einsum(
        "smh,h->sm", hidden, decode_second[0], preferred_element_type=jnp.float32
    )
    yields = jax.nn.softplus(output_logit)
    returned = lax.all_to_all(yields, ("band", "strip"), split_axis=0, concat_axis=0, tiled=True)
    own_yield = returned.reshape(-1)[destination]
    capacity_w = plant_capacity.astype(jnp.float32) * 0.001
    plant_power = capacity_w * own_yield
    power_sum = lax.psum(jnp.sum(plant_power), ("band", "strip"))
    fleet_yield = power_sum / float(plants_here * owner_count)
    return (final_field, plant_power, fleet_yield)


def solution(mesh):
    grid_fits = 32 * mesh.shape["strip"] == 256 and 64 * mesh.shape["band"] == 256
    return jax.shard_map(
        fast_body if grid_fits else body,
        mesh=mesh,
        in_specs=(
            P("band", "strip", None),
            P(),
            P(),
            P(),
            P(),
            P(),
            P(),
            P(("band", "strip")),
            P(("band", "strip"), None),
            P(("band", "strip")),
            P(("band", "strip"), None),
            P(("band", "strip"), None),
        ),
        out_specs=(P("band", "strip", None), P(("band", "strip")), P()),
        check_vma=False,
    )
```

```python
import jax
import jax.numpy as jnp
from jax import lax
from jax.experimental import pallas as pl
from jax.experimental.pallas import tpu as pltpu
from jax.sharding import PartitionSpec as P

HEADS = 8


EPS = 1e-06
TAU = 12.0
LOG2_E = 1.4426950408889634


def norm_rows(values, scale_factor):
    widened = values.astype(jnp.float32)
    return (
        widened
        * lax.rsqrt(jnp.mean(widened * widened, axis=-1, keepdims=True) + EPS)
        * scale_factor
    )


def heads_norm(values):
    leading = values.shape[:-1]
    split_up = values.reshape(leading + (HEADS, values.shape[-1] // HEADS))
    normed = split_up * lax.rsqrt(jnp.mean(split_up * split_up, axis=-1, keepdims=True) + EPS)
    return normed.reshape(values.shape)


def project(tokens_in, scale_factor, weight_qkv):
    leading = tokens_in.shape[:-1]
    model_width = tokens_in.shape[-1]
    head_width = model_width // HEADS
    normed = norm_rows(tokens_in, scale_factor).astype(jnp.bfloat16).reshape(-1, model_width)
    projected = jnp.dot(normed, weight_qkv, preferred_element_type=jnp.float32)
    query = heads_norm(projected[:, :model_width]) * (TAU / head_width)
    keys_part = heads_norm(projected[:, model_width : 2 * model_width])
    values_part = projected[:, 2 * model_width :]
    shaped = leading + (model_width,)
    return (
        query.astype(jnp.bfloat16).reshape(shaped),
        keys_part.astype(jnp.bfloat16).reshape(shaped),
        values_part.astype(jnp.bfloat16).reshape(shaped),
    )


def attend(query, keys_part, values_part):
    batch_size, length, model_width = query.shape
    head_width = model_width // HEADS

    def split_heads(tensor):
        return tensor.reshape(batch_size, length, HEADS, head_width).transpose(2, 0, 1, 3)

    def one_head(operands):
        query_rows, key_rows, value_rows = operands
        attention_scores = jnp.einsum(
            "zxe,zle->zxl", query_rows, key_rows, preferred_element_type=jnp.float32
        )
        weights = jnp.exp(attention_scores)
        row_total = jnp.sum(weights, axis=-1, keepdims=True)
        weights_bfloat = (weights / row_total).astype(jnp.bfloat16)
        return jnp.einsum(
            "pem,pmj->pej", weights_bfloat, value_rows, preferred_element_type=jnp.float32
        ).astype(jnp.bfloat16)

    context = lax.map(
        one_head, (split_heads(query), split_heads(keys_part), split_heads(values_part))
    )
    return context.transpose(1, 2, 0, 3).reshape(batch_size, length, model_width)


def finish(tokens_in, context, weight_out):
    model_width = tokens_in.shape[-1]
    mixed = jnp.dot(
        context.reshape(-1, model_width), weight_out, preferred_element_type=jnp.float32
    )
    return (tokens_in.astype(jnp.float32) + mixed.reshape(tokens_in.shape)).astype(jnp.bfloat16)


def mix_layer(tokens_in, scale_factor, weight_qkv, weight_out):
    query, keys_part, values_part = project(tokens_in, scale_factor, weight_qkv)
    return finish(tokens_in, attend(query, keys_part, values_part), weight_out)


def sequence_layer(x, gain, weight_qkv, weight_out, head_sum):
    length, width = x.shape
    head = width // HEADS
    pair = 2 * head
    scale = lax.rsqrt(jnp.mean(x * x, axis=-1, keepdims=True) + EPS)
    normed = (x * scale * gain).astype(jnp.bfloat16)
    lane = lax.broadcasted_iota(jnp.int32, (length, pair), 1)
    even = lane < head
    half = head_sum.shape[0]

    def head_scale(part):
        squares = (part * part).astype(jnp.bfloat16)
        sums = jnp.dot(squares, head_sum, preferred_element_type=jnp.float32)
        return part * lax.rsqrt(sums * (1.0 / head) + EPS)

    ones_e = jnp.where(even, 1.0, 0.0).astype(jnp.bfloat16)
    ones_o = jnp.where(even, 0.0, 1.0).astype(jnp.bfloat16)
    zero = jnp.zeros((length, pair), jnp.float32)
    contexts = []
    for start in range(0, width, half):
        wide = slice(start, start + half)
        query = jnp.dot(normed, weight_qkv[:, wide], preferred_element_type=jnp.float32)
        keys = jnp.dot(
            normed,
            weight_qkv[:, width + start : width + start + half],
            preferred_element_type=jnp.float32,
        )
        values = jnp.dot(
            normed,
            weight_qkv[:, 2 * width + start : 2 * width + start + half],
            preferred_element_type=jnp.float32,
        )
        query = (head_scale(query) * (TAU / head * LOG2_E)).astype(jnp.bfloat16)
        keys = head_scale(keys)
        for at in range(0, half, pair):
            k = keys[:, at : at + pair]
            v = values[:, at : at + pair]
            k_two = jnp.concatenate(
                [jnp.where(even, k, zero), jnp.where(even, zero, k)], axis=0
            ).astype(jnp.bfloat16)
            scores = lax.dot_general(
                query[:, at : at + pair],
                k_two,
                (((1,), (1,)), ((), ())),
                preferred_element_type=jnp.float32,
            )
            weights = jnp.exp2(scores).astype(jnp.bfloat16)
            v_two = jnp.concatenate(
                [
                    jnp.concatenate([jnp.where(even, v, zero).astype(jnp.bfloat16), ones_e], axis=1),
                    jnp.concatenate([jnp.where(even, zero, v).astype(jnp.bfloat16), ones_o], axis=1),
                ],
                axis=0,
            )
            mixed = jnp.dot(weights, v_two, preferred_element_type=jnp.float32)
            contexts.append((mixed[:, :pair] / mixed[:, pair:]).astype(jnp.bfloat16))
    context = jnp.concatenate(contexts, axis=1)
    return x + jnp.dot(context, weight_out[...], preferred_element_type=jnp.float32)


MESH = pl.DeviceIdType.MESH

def whole_kernel(
    cloud, row_gain, col_gain, cells, owners, capacity, second,
    row_qkv_in, row_out_in, col_qkv_in, col_out_in, first_in,
    final, power, fleet,
    rows_in, mixed, rows_out, cols_in, columns, cols_out, blocks_in, picks,
    sites_out, sites_in, listed_out, listed_in, yields_out, returned,
    field, placed, row_qkv, row_out, col_qkv, col_out, first, head_sum,
    rows_sent, rows_got, turn_sent, turn_got, cols_sent, cols_got, site_sems, done_sem, weight_sems,
):
    strips = lax.axis_size("strip")
    bands = lax.axis_size("band")
    devices = strips * bands
    strip = lax.axis_index("strip")
    band = lax.axis_index("band")
    me = band * strips + strip
    width = cloud.shape[2]
    length = columns.shape[1] // 4

    def wait_bytes(ref, sem):
        pltpu.make_async_copy(ref, ref, sem).wait()

    def split(number):
        return (number // strips, number % strips)

    weights = [
        pltpu.make_async_copy(source, target, weight_sems.at[number])
        for number, (source, target) in enumerate(
            (
                (row_qkv_in, row_qkv),
                (row_out_in, row_out),
                (col_qkv_in, col_qkv),
                (col_out_in, col_out),
                (first_in, first),
            )
        )
    ]
    barrier = pltpu.get_barrier_semaphore()

    @pl.loop(1, devices)
    def _(step):
        pl.semaphore_signal(
            barrier, inc=1, device_id=split((me + step) % devices), device_id_type=MESH
        )

    pl.semaphore_wait(barrier, devices - 1)

    @pl.loop(0, 4)
    def _(part):
        @pl.loop(1, strips)
        def _(step):
            to = (strip + step) % strips
            pltpu.make_async_remote_copy(
                src_ref=cloud.at[pl.ds(to * 8 + part * 2, 2)],
                dst_ref=rows_in.at[part, strip],
                send_sem=rows_sent.at[part],
                recv_sem=rows_got.at[part],
                device_id=(band, to),
                device_id_type=MESH,
            ).start()

        pltpu.make_async_copy(
            cloud.at[pl.ds(strip * 8 + part * 2, 2)], rows_in.at[part, strip], rows_got.at[part]
        ).start()

    for copy in weights:
        copy.start()
    head = width // HEADS
    head_sum[...] = jnp.where(
        lax.broadcasted_iota(jnp.int32, head_sum.shape, 0) // head
        == lax.broadcasted_iota(jnp.int32, head_sum.shape, 1) // head,
        1.0,
        0.0,
    ).astype(jnp.bfloat16)

    plants = cells.shape[1]
    slots = 8
    owner_hot = lax.broadcasted_iota(jnp.int32, (devices, plants), 0) == owners[...]
    owner_one = jnp.where(owner_hot, 1.0, 0.0)
    before = (
        lax.broadcasted_iota(jnp.int32, (plants, plants), 0)
        < lax.broadcasted_iota(jnp.int32, (plants, plants), 1)
    )
    earlier = jnp.dot(
        owner_one.astype(jnp.bfloat16),
        jnp.where(before, 1.0, 0.0).astype(jnp.bfloat16),
        preferred_element_type=jnp.float32,
    )
    slot = jnp.sum(owner_one * earlier, axis=0, keepdims=True).astype(jnp.int32)
    spot = owners[...] * slots + slot
    place = jnp.where(
        lax.broadcasted_iota(jnp.int32, (devices * slots, plants), 0) == spot, 1.0, 0.0
    )
    lane = lax.broadcasted_iota(jnp.int32, (devices, slots, 128), 2)
    own_lane = lane == lax.broadcasted_iota(jnp.int32, (devices, slots, 128), 1)

    def to_lanes(column):
        wide = jnp.broadcast_to(column, (devices * slots, 128)).reshape(devices, slots, 128)
        return jnp.sum(jnp.where(own_lane, wide, 0.0), axis=1, keepdims=True)

    kilowatts = capacity[...].astype(jnp.float32)
    listed_out[...] = to_lanes(jnp.sum(place * kilowatts, axis=1, keepdims=True))

    @pl.loop(1, devices)
    def _(step):
        to = (me + step) % devices
        pltpu.make_async_remote_copy(
            src_ref=listed_out.at[to],
            dst_ref=listed_in.at[me],
            send_sem=site_sems.at[4],
            recv_sem=site_sems.at[5],
            device_id=split(to),
            device_id_type=MESH,
        ).start()

    pltpu.make_async_copy(listed_out.at[me], listed_in.at[me], site_sems.at[5]).start()

    rows_here = cloud.shape[0]
    cols_here = cloud.shape[1]
    cell_row = cells[...] // cols_here
    cell_col = cells[...] % cols_here
    in_block = cell_col // 8 * rows_here + cell_row
    block = cell_col % 2 * 4 + cell_col % 8 // 2

    @pl.loop(0, 8)
    def _(col):
        at_cell = jnp.where(
            lax.broadcasted_iota(jnp.int32, (length, plants), 0)
            == jnp.where(block == col, in_block, -1),
            1.0,
            0.0,
        )
        picks[col] = lax.dot_general(
            place.astype(jnp.bfloat16),
            at_cell.astype(jnp.bfloat16),
            (((1,), (1,)), ((), ())),
            preferred_element_type=jnp.float32,
        ).astype(jnp.bfloat16)

    def send_turn(parity, part):
        @pl.loop(1, devices)
        def _(step):
            to_band, to_strip = split((me + step) % devices)
            pltpu.make_async_remote_copy(
                src_ref=rows_out.at[part, parity, to_strip * bands + to_band],
                dst_ref=cols_in.at[parity, part, me],
                send_sem=turn_sent.at[parity, part],
                recv_sem=turn_got.at[parity, part],
                device_id=(to_band, to_strip),
                device_id_type=MESH,
            ).start()

        pltpu.make_async_copy(
            rows_out.at[part, parity, strip * bands + band],
            cols_in.at[parity, part, me],
            turn_got.at[parity, part],
        ).start()

    def turn_left(parity, part):
        wait_bytes(cols_in.at[parity, part, pl.ds(0, devices - 1)], turn_sent.at[parity, part])

    weights[0].wait()
    weights[1].wait()

    @pl.loop(0, 2)
    def _(part):
        @pl.loop(0, 4)
        def _(row):
            pair = part * 2 + row // 2

            @pl.when(row % 2 == 0)
            def _():
                wait_bytes(rows_in.at[pair], rows_got.at[pair])

            x = rows_in[pair, :, row % 2].astype(jnp.float32).reshape(length, width)
            y = sequence_layer(x, row_gain[...], row_qkv, row_out, head_sum[...])
            for lanes in range(0, width, 128):
                mixed[lanes // 128, :, pl.ds(pl.multiple_of(row * 8, 8), 8), :] = y[
                    :, lanes : lanes + 128
                ].reshape(devices, 8, 128)

        for parity in range(2):
            for lanes in range(0, width, 128):
                taken = mixed.at[lanes // 128].reshape(devices * 32, 128)[
                    pl.ds(parity, devices * 16, stride=2), :
                ]
                rows_out[part, parity, :, :, lanes : lanes + 128] = (
                    taken.astype(jnp.bfloat16).reshape(devices, 16, 128)
                )

        send_turn(0, part)

    for part in range(2):
        turn_left(0, part)
        send_turn(1, part)
    weights[2].wait()
    weights[3].wait()

    @pl.loop(0, 2)
    def _(parity):
        for part in range(2):
            wait_bytes(cols_in.at[parity, part], turn_got.at[parity, part])

            @pl.loop(0, devices)
            def _(src):
                at = pl.multiple_of(src * 32 + part * 16, 16)
                for lanes in range(0, width, 128):
                    columns[lanes // 128, pl.ds(at, 16), :] = cols_in[
                        parity, part, src, :, lanes : lanes + 128
                    ].astype(jnp.float32)

        @pl.loop(0, 4)
        def _(number):
            x = jnp.concatenate(
                [
                    columns[lanes, pl.ds(number, length, stride=4), :]
                    for lanes in range(width // 128)
                ],
                axis=1,
            )
            y = sequence_layer(x, col_gain[...], col_qkv, col_out, head_sum[...])
            col = parity * 4 + number
            cols_out[col] = y.astype(jnp.bfloat16).reshape(bands, length // bands, width)

            @pl.loop(1, bands)
            def _(step):
                to = (band + step) % bands
                pltpu.make_async_remote_copy(
                    src_ref=cols_out.at[col, to],
                    dst_ref=blocks_in.at[col, band],
                    send_sem=cols_sent.at[col],
                    recv_sem=cols_got.at[col],
                    device_id=(to, strip),
                    device_id_type=MESH,
                ).start()

            pltpu.make_async_copy(
                cols_out.at[col, band], blocks_in.at[col, band], cols_got.at[col]
            ).start()

    sites = jnp.zeros((devices * slots, width), jnp.float32)
    for col in range(8):
        wait_bytes(blocks_in.at[col], cols_got.at[col])
        sites = sites + jnp.dot(
            picks[col],
            blocks_in[col].reshape(length, width),
            preferred_element_type=jnp.float32,
        )
        for src in range(4):
            at = src * 8 + 2 * (col % 4) + col // 4
            for lanes in range(0, width, 128):
                field[lanes // 128, pl.ds(at, rows_here, stride=cols_here), :] = blocks_in[
                    col, src, :, lanes : lanes + 128
                ].astype(jnp.float32)
    sites = sites.reshape(devices, slots, width)
    half = width // 2
    sites_out[...] = jnp.concatenate([sites[:, :, :half], sites[:, :, half:]], axis=1).astype(
        jnp.bfloat16
    )

    @pl.loop(1, devices)
    def _(step):
        to = (me + step) % devices
        pltpu.make_async_remote_copy(
            src_ref=sites_out.at[to],
            dst_ref=sites_in.at[me],
            send_sem=site_sems.at[0],
            recv_sem=site_sems.at[1],
            device_id=split(to),
            device_id_type=MESH,
        ).start()

    pltpu.make_async_copy(sites_out.at[me], sites_in.at[me], site_sems.at[1]).start()

    @pl.loop(0, rows_here // 8)
    def _(row):
        tokens = pl.ds(pl.multiple_of(row * 8 * cols_here, 256), 8 * cols_here)
        for lanes in range(0, width, 128):
            placed[pl.ds(row * 8, 8), :, lanes : lanes + 128] = (
                field[lanes // 128, tokens, :].astype(jnp.bfloat16).reshape(8, cols_here, 128)
            )

    pltpu.make_async_copy(placed, final, done_sem).start()
    weights[4].wait()
    wait_bytes(listed_in, site_sems.at[5])
    wait_bytes(sites_in, site_sems.at[1])

    arrived = sites_in[...].astype(jnp.float32)
    hidden = jnp.dot(
        arrived[:, :slots].reshape(devices * slots, half).astype(jnp.bfloat16),
        first[:half, :],
        preferred_element_type=jnp.float32,
    ) + jnp.dot(
        arrived[:, slots:].reshape(devices * slots, half).astype(jnp.bfloat16),
        first[half:, :],
        preferred_element_type=jnp.float32,
    )
    hidden = jax.nn.gelu(hidden).astype(jnp.bfloat16).astype(jnp.float32)
    logit = jnp.sum(hidden * second[...].astype(jnp.float32), axis=1, keepdims=True)
    yields = to_lanes(jnp.maximum(logit, 0.0) + jnp.log1p(jnp.exp(-jnp.abs(logit))))
    total = jnp.sum(yields * listed_in[...] * 0.001, axis=(0, 2), keepdims=True)
    yields_out[...] = jnp.where(lane[:, :1] == slots, total, yields)

    @pl.loop(1, devices)
    def _(step):
        to = (me + step) % devices
        pltpu.make_async_remote_copy(
            src_ref=yields_out.at[to],
            dst_ref=returned.at[me],
            send_sem=site_sems.at[2],
            recv_sem=site_sems.at[3],
            device_id=split(to),
            device_id_type=MESH,
        ).start()

    pltpu.make_async_copy(yields_out.at[me], returned.at[me], site_sems.at[3]).start()

    for pair in range(4):
        wait_bytes(rows_in.at[pair, pl.ds(0, strips - 1)], rows_sent.at[pair])
    for part in range(2):
        turn_left(1, part)
    for col in range(8):
        wait_bytes(cols_out.at[col, pl.ds(0, bands - 1)], cols_sent.at[col])
    wait_bytes(sites_out.at[pl.ds(0, devices - 1)], site_sems.at[0])
    wait_bytes(listed_out.at[pl.ds(0, devices - 1)], site_sems.at[4])

    wait_bytes(returned, site_sems.at[3])
    back = returned[...].reshape(devices, 128)
    by_slot = lax.dot_general(
        back,
        owner_one,
        (((0,), (0,)), ((), ())),
        precision=lax.Precision.HIGHEST,
        preferred_element_type=jnp.float32,
    )
    own = lax.broadcasted_iota(jnp.int32, (128, plants), 0) == slot
    power[...] = kilowatts * 0.001 * jnp.sum(jnp.where(own, by_slot, 0.0), axis=0, keepdims=True)
    sums = jnp.sum(jnp.where(lane[:, 0] == slots, back, 0.0), axis=(0, 1), keepdims=True)
    fleet[...] = jnp.broadcast_to(sums / float(plants * devices), fleet.shape)
    wait_bytes(yields_out.at[pl.ds(0, devices - 1)], site_sems.at[2])
    wait_bytes(placed, done_sem)


def fast_body(
    cloud_field,
    row_gain,
    row_qkv,
    row_out,
    col_gain,
    col_qkv,
    col_out,
    plant_cell,
    plant_decoder_device,
    plant_capacity,
    decode_first,
    decode_second,
):
    rows_here, cols_here, width = cloud_field.shape
    strips = lax.axis_size("strip")
    bands = lax.axis_size("band")
    devices = bands * strips
    length = cols_here * strips
    plants_here = plant_cell.shape[0]

    vmem = pl.BlockSpec(memory_space=pltpu.VMEM)
    anywhere = pl.BlockSpec(memory_space=pl.ANY)
    half = 4 * (width // HEADS)
    bf16 = jnp.bfloat16
    final_field, power, fleet = pl.pallas_call(
        whole_kernel,
        out_shape=(
            jax.ShapeDtypeStruct(cloud_field.shape, bf16),
            jax.ShapeDtypeStruct((1, plants_here), jnp.float32),
            jax.ShapeDtypeStruct((1, 128), jnp.float32),
        ),
        in_specs=[anywhere] + [vmem] * 6 + [anywhere] * 5,
        out_specs=(anywhere, vmem, vmem),
        scratch_shapes=[
            pltpu.VMEM((4, strips, 2, cols_here, width), bf16),
            pltpu.VMEM((width // 128, devices, 32, 128), jnp.float32),
            pltpu.VMEM((2, 2, devices, 16, width), bf16),
            pltpu.VMEM((2, 2, devices, 16, width), bf16),
            pltpu.VMEM((width // 128, 4 * length, 128), jnp.float32),
            pltpu.VMEM((8, bands, length // bands, width), bf16),
            pltpu.VMEM((8, bands, length // bands, width), bf16),
            pltpu.VMEM((8, devices * 8, length), bf16),
            pltpu.VMEM((devices, 16, width // 2), bf16),
            pltpu.VMEM((devices, 16, width // 2), bf16),
            pltpu.VMEM((devices, 1, 128), jnp.float32),
            pltpu.VMEM((devices, 1, 128), jnp.float32),
            pltpu.VMEM((devices, 1, 128), jnp.float32),
            pltpu.VMEM((devices, 1, 128), jnp.float32),
            pltpu.VMEM((width // 128, rows_here * cols_here, 128), jnp.float32),
            pltpu.VMEM(cloud_field.shape, bf16),
            pltpu.VMEM(row_qkv.shape, bf16),
            pltpu.VMEM(row_out.shape, bf16),
            pltpu.VMEM(col_qkv.shape, bf16),
            pltpu.VMEM(col_out.shape, bf16),
            pltpu.VMEM(decode_first.shape, bf16),
            pltpu.VMEM((half, half), bf16),
            pltpu.SemaphoreType.DMA((4,)),
            pltpu.SemaphoreType.DMA((4,)),
            pltpu.SemaphoreType.DMA((2, 2)),
            pltpu.SemaphoreType.DMA((2, 2)),
            pltpu.SemaphoreType.DMA((8,)),
            pltpu.SemaphoreType.DMA((8,)),
            pltpu.SemaphoreType.DMA((6,)),
            pltpu.SemaphoreType.DMA,
            pltpu.SemaphoreType.DMA((5,)),
        ],
        compiler_params=pltpu.CompilerParams(
            collective_id=0, has_side_effects=True, vmem_limit_bytes=56 * 1024 * 1024
        ),
        cost_estimate=pl.CostEstimate(
            flops=4 * rows_here * cols_here * width * (4 * width + 2 * length),
            bytes_accessed=8 * cloud_field.size,
            transcendentals=2 * rows_here * cols_here * HEADS * length,
        ),
    )(
        cloud_field,
        row_gain.reshape(1, width),
        col_gain.reshape(1, width),
        plant_cell.reshape(1, plants_here),
        plant_decoder_device.reshape(1, plants_here),
        plant_capacity.reshape(1, plants_here),
        decode_second,
        row_qkv,
        row_out,
        col_qkv,
        col_out,
        decode_first,
    )
    return (final_field, power[0], fleet[0, 0])


def body(
    cloud_field,
    row_gain,
    row_qkv,
    row_out,
    col_gain,
    col_qkv,
    col_out,
    plant_cell,
    plant_decoder_device,
    plant_capacity,
    decode_first,
    decode_second,
):
    rows_here, cols_here, model_width = cloud_field.shape
    strips = lax.axis_size("strip")
    bands = lax.axis_size("band")
    owner_count = bands * strips
    row_share = rows_here // strips
    col_share = cols_here // bands
    shape_send = (strips, row_share, cols_here, model_width)
    mixed_rows = mix_layer(
        lax.all_to_all(
            cloud_field.reshape(shape_send), "strip", split_axis=0, concat_axis=2, tiled=True
        )[0],
        row_gain,
        row_qkv,
        row_out,
    )[None]
    after_rows = lax.all_to_all(
        mixed_rows, "strip", split_axis=2, concat_axis=0, tiled=True
    ).reshape(rows_here, cols_here, model_width)
    turned = lax.all_to_all(
        after_rows.reshape(rows_here, bands, col_share, model_width),
        "band",
        split_axis=1,
        concat_axis=0,
        tiled=True,
    )[:, 0].transpose(1, 0, 2)
    mixed_cols = mix_layer(turned, col_gain, col_qkv, col_out)
    columns_done = mixed_cols.transpose(1, 0, 2)[:, None]
    final_field = lax.all_to_all(
        columns_done, "band", split_axis=0, concat_axis=1, tiled=True
    ).reshape(rows_here, cols_here, model_width)
    plants_here = plant_cell.shape[0]
    most_slots = 2 * plants_here // owner_count
    flat_field = final_field.reshape(rows_here * cols_here, model_width)
    features = flat_field[plant_cell]
    owners = plant_decoder_device[:, 0]
    one_hot = (owners[:, None] == jnp.arange(owner_count, dtype=jnp.int32)[None, :]).astype(
        jnp.int32
    )
    running = jnp.cumsum(one_hot, axis=0)
    slot_of = jnp.sum(one_hot * (running - 1), axis=1)
    destination = owners * most_slots + slot_of
    send_buffer = (
        jnp.zeros((owner_count * most_slots, model_width), jnp.bfloat16)
        .at[destination]
        .set(features)
    )
    send_buffer = send_buffer.reshape(owner_count, most_slots, model_width)
    hidden = jax.nn.gelu(
        jnp.einsum(
            "smd,dh->smh",
            lax.all_to_all(send_buffer, ("band", "strip"), split_axis=0, concat_axis=0, tiled=True),
            decode_first,
            preferred_element_type=jnp.float32,
        )
    ).astype(jnp.bfloat16)
    output_logit = jnp.einsum(
        "smh,h->sm", hidden, decode_second[0], preferred_element_type=jnp.float32
    )
    yields = jax.nn.softplus(output_logit)
    returned = lax.all_to_all(yields, ("band", "strip"), split_axis=0, concat_axis=0, tiled=True)
    own_yield = returned.reshape(-1)[destination]
    capacity_w = plant_capacity.astype(jnp.float32) * 0.001
    plant_power = capacity_w * own_yield
    power_sum = lax.psum(jnp.sum(plant_power), ("band", "strip"))
    fleet_yield = power_sum / float(plants_here * owner_count)
    return (final_field, plant_power, fleet_yield)


def solution(mesh):
    grid_fits = 32 * mesh.shape["strip"] == 256 and 64 * mesh.shape["band"] == 256
    return jax.shard_map(
        fast_body if grid_fits else body,
        mesh=mesh,
        in_specs=(
            P("band", "strip", None),
            P(),
            P(),
            P(),
            P(),
            P(),
            P(),
            P(("band", "strip")),
            P(("band", "strip"), None),
            P(("band", "strip")),
            P(("band", "strip"), None),
            P(("band", "strip"), None),
        ),
        out_specs=(P("band", "strip", None), P(("band", "strip")), P()),
        check_vma=False,
    )
```

```python
import jax
import jax.numpy as jnp
from jax import lax
from jax.experimental import pallas as pl
from jax.experimental.pallas import tpu as pltpu
from jax.sharding import PartitionSpec as P

HEADS = 8


EPS = 1e-06
TAU = 12.0
LOG2_E = 1.4426950408889634


def norm_rows(values, scale_factor):
    widened = values.astype(jnp.float32)
    return (
        widened
        * lax.rsqrt(jnp.mean(widened * widened, axis=-1, keepdims=True) + EPS)
        * scale_factor
    )


def heads_norm(values):
    leading = values.shape[:-1]
    split_up = values.reshape(leading + (HEADS, values.shape[-1] // HEADS))
    normed = split_up * lax.rsqrt(jnp.mean(split_up * split_up, axis=-1, keepdims=True) + EPS)
    return normed.reshape(values.shape)


def project(tokens_in, scale_factor, weight_qkv):
    leading = tokens_in.shape[:-1]
    model_width = tokens_in.shape[-1]
    head_width = model_width // HEADS
    normed = norm_rows(tokens_in, scale_factor).astype(jnp.bfloat16).reshape(-1, model_width)
    projected = jnp.dot(normed, weight_qkv, preferred_element_type=jnp.float32)
    query = heads_norm(projected[:, :model_width]) * (TAU / head_width)
    keys_part = heads_norm(projected[:, model_width : 2 * model_width])
    values_part = projected[:, 2 * model_width :]
    shaped = leading + (model_width,)
    return (
        query.astype(jnp.bfloat16).reshape(shaped),
        keys_part.astype(jnp.bfloat16).reshape(shaped),
        values_part.astype(jnp.bfloat16).reshape(shaped),
    )


def attend(query, keys_part, values_part):
    batch_size, length, model_width = query.shape
    head_width = model_width // HEADS

    def split_heads(tensor):
        return tensor.reshape(batch_size, length, HEADS, head_width).transpose(2, 0, 1, 3)

    def one_head(operands):
        query_rows, key_rows, value_rows = operands
        attention_scores = jnp.einsum(
            "zxe,zle->zxl", query_rows, key_rows, preferred_element_type=jnp.float32
        )
        weights = jnp.exp(attention_scores)
        row_total = jnp.sum(weights, axis=-1, keepdims=True)
        weights_bfloat = (weights / row_total).astype(jnp.bfloat16)
        return jnp.einsum(
            "pem,pmj->pej", weights_bfloat, value_rows, preferred_element_type=jnp.float32
        ).astype(jnp.bfloat16)

    context = lax.map(
        one_head, (split_heads(query), split_heads(keys_part), split_heads(values_part))
    )
    return context.transpose(1, 2, 0, 3).reshape(batch_size, length, model_width)


def finish(tokens_in, context, weight_out):
    model_width = tokens_in.shape[-1]
    mixed = jnp.dot(
        context.reshape(-1, model_width), weight_out, preferred_element_type=jnp.float32
    )
    return (tokens_in.astype(jnp.float32) + mixed.reshape(tokens_in.shape)).astype(jnp.bfloat16)


def mix_layer(tokens_in, scale_factor, weight_qkv, weight_out):
    query, keys_part, values_part = project(tokens_in, scale_factor, weight_qkv)
    return finish(tokens_in, attend(query, keys_part, values_part), weight_out)


def sequence_layer(x, gain, weight_qkv, weight_out, head_sum):
    length, width = x.shape
    head = width // HEADS
    pair = 2 * head
    scale = lax.rsqrt(jnp.mean(x * x, axis=-1, keepdims=True) + EPS)
    normed = (x * scale * gain).astype(jnp.bfloat16)
    lane = lax.broadcasted_iota(jnp.int32, (length, pair), 1)
    even = lane < head
    half = head_sum.shape[0]

    def head_scale(part):
        squares = (part * part).astype(jnp.bfloat16)
        sums = jnp.dot(squares, head_sum, preferred_element_type=jnp.float32)
        return part * lax.rsqrt(sums * (1.0 / head) + EPS)

    ones_e = jnp.where(even, 1.0, 0.0).astype(jnp.bfloat16)
    ones_o = jnp.where(even, 0.0, 1.0).astype(jnp.bfloat16)
    zero = jnp.zeros((length, pair), jnp.float32)
    contexts = []
    for start in range(0, width, half):
        wide = slice(start, start + half)
        query = jnp.dot(normed, weight_qkv[:, wide], preferred_element_type=jnp.float32)
        keys = jnp.dot(
            normed,
            weight_qkv[:, width + start : width + start + half],
            preferred_element_type=jnp.float32,
        )
        values = jnp.dot(
            normed,
            weight_qkv[:, 2 * width + start : 2 * width + start + half],
            preferred_element_type=jnp.float32,
        )
        query = (head_scale(query) * (TAU / head * LOG2_E)).astype(jnp.bfloat16)
        keys = head_scale(keys)
        for at in range(0, half, pair):
            k = keys[:, at : at + pair]
            v = values[:, at : at + pair]
            k_two = jnp.concatenate(
                [jnp.where(even, k, zero), jnp.where(even, zero, k)], axis=0
            ).astype(jnp.bfloat16)
            scores = lax.dot_general(
                query[:, at : at + pair],
                k_two,
                (((1,), (1,)), ((), ())),
                preferred_element_type=jnp.float32,
            )
            weights = jnp.exp2(scores).astype(jnp.bfloat16)
            v_two = jnp.concatenate(
                [
                    jnp.concatenate([jnp.where(even, v, zero).astype(jnp.bfloat16), ones_e], axis=1),
                    jnp.concatenate([jnp.where(even, zero, v).astype(jnp.bfloat16), ones_o], axis=1),
                ],
                axis=0,
            )
            mixed = jnp.dot(weights, v_two, preferred_element_type=jnp.float32)
            contexts.append((mixed[:, :pair] / mixed[:, pair:]).astype(jnp.bfloat16))
    context = jnp.concatenate(contexts, axis=1)
    return x + jnp.dot(context, weight_out[...], preferred_element_type=jnp.float32)


MESH = pl.DeviceIdType.MESH

def whole_kernel(
    cloud, row_gain, col_gain, cells, owners, capacity, second,
    row_qkv_in, row_out_in, col_qkv_in, col_out_in, first_in,
    final, power, fleet,
    rows_in, mixed, rows_out, cols_in, columns, cols_out, blocks_in, picks,
    sites_out, sites_in, listed_out, listed_in, yields_out, returned,
    field, placed, row_qkv, row_out, col_qkv, col_out, first, head_sum,
    rows_sent, rows_got, turn_sent, turn_got, cols_sent, cols_got, site_sems, done_sem, weight_sems,
):
    strips = lax.axis_size("strip")
    bands = lax.axis_size("band")
    devices = strips * bands
    strip = lax.axis_index("strip")
    band = lax.axis_index("band")
    me = band * strips + strip
    width = cloud.shape[2]
    length = columns.shape[1] // 4

    def wait_bytes(ref, sem):
        pltpu.make_async_copy(ref, ref, sem).wait()

    def split(number):
        return (number // strips, number % strips)

    weights = [
        pltpu.make_async_copy(source, target, weight_sems.at[number])
        for number, (source, target) in enumerate(
            (
                (row_qkv_in, row_qkv),
                (row_out_in, row_out),
                (col_qkv_in, col_qkv),
                (col_out_in, col_out),
                (first_in, first),
            )
        )
    ]
    barrier = pltpu.get_barrier_semaphore()

    @pl.loop(1, devices)
    def _(step):
        pl.semaphore_signal(
            barrier, inc=1, device_id=split((me + step) % devices), device_id_type=MESH
        )

    pl.semaphore_wait(barrier, devices - 1)

    def send_rows(part):
        @pl.loop(1, strips)
        def _(step):
            to = (strip + step) % strips
            pltpu.make_async_remote_copy(
                src_ref=cloud.at[pl.ds(to * 8 + part * 2, 2)],
                dst_ref=rows_in.at[part, strip],
                send_sem=rows_sent.at[part],
                recv_sem=rows_got.at[part],
                device_id=(band, to),
                device_id_type=MESH,
            ).start()

        pltpu.make_async_copy(
            cloud.at[pl.ds(strip * 8 + part * 2, 2)], rows_in.at[part, strip], rows_got.at[part]
        ).start()

    send_rows(0)
    send_rows(1)
    for copy in weights:
        copy.start()
    head = width // HEADS
    head_sum[...] = jnp.where(
        lax.broadcasted_iota(jnp.int32, head_sum.shape, 0) // head
        == lax.broadcasted_iota(jnp.int32, head_sum.shape, 1) // head,
        1.0,
        0.0,
    ).astype(jnp.bfloat16)

    plants = cells.shape[1]
    slots = 8
    owner_hot = lax.broadcasted_iota(jnp.int32, (devices, plants), 0) == owners[...]
    owner_one = jnp.where(owner_hot, 1.0, 0.0)
    before = (
        lax.broadcasted_iota(jnp.int32, (plants, plants), 0)
        < lax.broadcasted_iota(jnp.int32, (plants, plants), 1)
    )
    earlier = jnp.dot(
        owner_one.astype(jnp.bfloat16),
        jnp.where(before, 1.0, 0.0).astype(jnp.bfloat16),
        preferred_element_type=jnp.float32,
    )
    slot = jnp.sum(owner_one * earlier, axis=0, keepdims=True).astype(jnp.int32)
    spot = owners[...] * slots + slot
    place = jnp.where(
        lax.broadcasted_iota(jnp.int32, (devices * slots, plants), 0) == spot, 1.0, 0.0
    )
    lane = lax.broadcasted_iota(jnp.int32, (devices, slots, 128), 2)
    own_lane = lane == lax.broadcasted_iota(jnp.int32, (devices, slots, 128), 1)

    def to_lanes(column):
        wide = jnp.broadcast_to(column, (devices * slots, 128)).reshape(devices, slots, 128)
        return jnp.sum(jnp.where(own_lane, wide, 0.0), axis=1, keepdims=True)

    kilowatts = capacity[...].astype(jnp.float32)
    listed_out[...] = to_lanes(jnp.sum(place * kilowatts, axis=1, keepdims=True))

    @pl.loop(1, devices)
    def _(step):
        to = (me + step) % devices
        pltpu.make_async_remote_copy(
            src_ref=listed_out.at[to],
            dst_ref=listed_in.at[me],
            send_sem=site_sems.at[4],
            recv_sem=site_sems.at[5],
            device_id=split(to),
            device_id_type=MESH,
        ).start()

    pltpu.make_async_copy(listed_out.at[me], listed_in.at[me], site_sems.at[5]).start()

    rows_here = cloud.shape[0]
    cols_here = cloud.shape[1]
    cell_row = cells[...] // cols_here
    cell_col = cells[...] % cols_here
    in_block = cell_col // 8 * rows_here + cell_row
    block = cell_col % 2 * 4 + cell_col % 8 // 2

    @pl.loop(0, 8)
    def _(col):
        at_cell = jnp.where(
            lax.broadcasted_iota(jnp.int32, (length, plants), 0)
            == jnp.where(block == col, in_block, -1),
            1.0,
            0.0,
        )
        picks[col] = lax.dot_general(
            place.astype(jnp.bfloat16),
            at_cell.astype(jnp.bfloat16),
            (((1,), (1,)), ((), ())),
            preferred_element_type=jnp.float32,
        ).astype(jnp.bfloat16)

    def send_turn(parity, part):
        @pl.loop(1, devices)
        def _(step):
            to_band, to_strip = split((me + step) % devices)
            pltpu.make_async_remote_copy(
                src_ref=rows_out.at[part, parity, to_strip * bands + to_band],
                dst_ref=cols_in.at[parity, part, me],
                send_sem=turn_sent.at[parity, part],
                recv_sem=turn_got.at[parity, part],
                device_id=(to_band, to_strip),
                device_id_type=MESH,
            ).start()

        pltpu.make_async_copy(
            rows_out.at[part, parity, strip * bands + band],
            cols_in.at[parity, part, me],
            turn_got.at[parity, part],
        ).start()

    def turn_left(parity, part):
        wait_bytes(cols_in.at[parity, part, pl.ds(0, devices - 1)], turn_sent.at[parity, part])

    weights[0].wait()
    weights[1].wait()

    @pl.loop(0, 2)
    def _(part):
        @pl.loop(0, 4)
        def _(row):
            pair = part * 2 + row // 2

            @pl.when((row % 2 == 0) & (part == 0))
            def _():
                wait_bytes(rows_in.at[pair, pl.ds(0, strips - 1)], rows_sent.at[pair])
                send_rows(pair + 2)

            @pl.when(row % 2 == 0)
            def _():
                wait_bytes(rows_in.at[pair], rows_got.at[pair])

            x = rows_in[pair, :, row % 2].astype(jnp.float32).reshape(length, width)
            y = sequence_layer(x, row_gain[...], row_qkv, row_out, head_sum[...])
            for lanes in range(0, width, 128):
                mixed[lanes // 128, :, pl.ds(pl.multiple_of(row * 8, 8), 8), :] = y[
                    :, lanes : lanes + 128
                ].reshape(devices, 8, 128)

        for parity in range(2):
            for lanes in range(0, width, 128):
                taken = mixed.at[lanes // 128].reshape(devices * 32, 128)[
                    pl.ds(parity, devices * 16, stride=2), :
                ]
                rows_out[part, parity, :, :, lanes : lanes + 128] = (
                    taken.astype(jnp.bfloat16).reshape(devices, 16, 128)
                )

        send_turn(0, part)

    for part in range(2):
        turn_left(0, part)
        send_turn(1, part)
    weights[2].wait()
    weights[3].wait()

    @pl.loop(0, 2)
    def _(parity):
        for part in range(2):
            wait_bytes(cols_in.at[parity, part], turn_got.at[parity, part])

            @pl.loop(0, devices)
            def _(src):
                at = pl.multiple_of(src * 32 + part * 16, 16)
                for lanes in range(0, width, 128):
                    columns[lanes // 128, pl.ds(at, 16), :] = cols_in[
                        parity, part, src, :, lanes : lanes + 128
                    ].astype(jnp.float32)

        @pl.loop(0, 4)
        def _(number):
            x = jnp.concatenate(
                [
                    columns[lanes, pl.ds(number, length, stride=4), :]
                    for lanes in range(width // 128)
                ],
                axis=1,
            )
            y = sequence_layer(x, col_gain[...], col_qkv, col_out, head_sum[...])
            col = parity * 4 + number
            cols_out[col] = y.astype(jnp.bfloat16).reshape(bands, length // bands, width)

            @pl.loop(1, bands)
            def _(step):
                to = (band + step) % bands
                pltpu.make_async_remote_copy(
                    src_ref=cols_out.at[col, to],
                    dst_ref=blocks_in.at[col, band],
                    send_sem=cols_sent.at[col],
                    recv_sem=cols_got.at[col],
                    device_id=(to, strip),
                    device_id_type=MESH,
                ).start()

            pltpu.make_async_copy(
                cols_out.at[col, band], blocks_in.at[col, band], cols_got.at[col]
            ).start()

    sites = jnp.zeros((devices * slots, width), jnp.float32)
    for col in range(8):
        wait_bytes(blocks_in.at[col], cols_got.at[col])
        sites = sites + jnp.dot(
            picks[col],
            blocks_in[col].reshape(length, width),
            preferred_element_type=jnp.float32,
        )
        for src in range(4):
            at = src * 8 + 2 * (col % 4) + col // 4
            for lanes in range(0, width, 128):
                field[lanes // 128, pl.ds(at, rows_here, stride=cols_here), :] = blocks_in[
                    col, src, :, lanes : lanes + 128
                ].astype(jnp.float32)
    sites = sites.reshape(devices, slots, width)
    half = width // 2
    sites_out[...] = jnp.concatenate([sites[:, :, :half], sites[:, :, half:]], axis=1).astype(
        jnp.bfloat16
    )

    @pl.loop(1, devices)
    def _(step):
        to = (me + step) % devices
        pltpu.make_async_remote_copy(
            src_ref=sites_out.at[to],
            dst_ref=sites_in.at[me],
            send_sem=site_sems.at[0],
            recv_sem=site_sems.at[1],
            device_id=split(to),
            device_id_type=MESH,
        ).start()

    pltpu.make_async_copy(sites_out.at[me], sites_in.at[me], site_sems.at[1]).start()

    @pl.loop(0, rows_here // 8)
    def _(row):
        tokens = pl.ds(pl.multiple_of(row * 8 * cols_here, 256), 8 * cols_here)
        for lanes in range(0, width, 128):
            placed[pl.ds(row * 8, 8), :, lanes : lanes + 128] = (
                field[lanes // 128, tokens, :].astype(jnp.bfloat16).reshape(8, cols_here, 128)
            )

    pltpu.make_async_copy(placed, final, done_sem).start()
    weights[4].wait()
    wait_bytes(listed_in, site_sems.at[5])
    wait_bytes(sites_in, site_sems.at[1])

    arrived = sites_in[...].astype(jnp.float32)
    hidden = jnp.dot(
        arrived[:, :slots].reshape(devices * slots, half).astype(jnp.bfloat16),
        first[:half, :],
        preferred_element_type=jnp.float32,
    ) + jnp.dot(
        arrived[:, slots:].reshape(devices * slots, half).astype(jnp.bfloat16),
        first[half:, :],
        preferred_element_type=jnp.float32,
    )
    hidden = jax.nn.gelu(hidden).astype(jnp.bfloat16).astype(jnp.float32)
    logit = jnp.sum(hidden * second[...].astype(jnp.float32), axis=1, keepdims=True)
    yields = to_lanes(jnp.maximum(logit, 0.0) + jnp.log1p(jnp.exp(-jnp.abs(logit))))
    total = jnp.sum(yields * listed_in[...] * 0.001, axis=(0, 2), keepdims=True)
    yields_out[...] = jnp.where(lane[:, :1] == slots, total, yields)

    @pl.loop(1, devices)
    def _(step):
        to = (me + step) % devices
        pltpu.make_async_remote_copy(
            src_ref=yields_out.at[to],
            dst_ref=returned.at[me],
            send_sem=site_sems.at[2],
            recv_sem=site_sems.at[3],
            device_id=split(to),
            device_id_type=MESH,
        ).start()

    pltpu.make_async_copy(yields_out.at[me], returned.at[me], site_sems.at[3]).start()

    for pair in range(2, 4):
        wait_bytes(rows_in.at[pair, pl.ds(0, strips - 1)], rows_sent.at[pair])
    for part in range(2):
        turn_left(1, part)
    for col in range(8):
        wait_bytes(cols_out.at[col, pl.ds(0, bands - 1)], cols_sent.at[col])
    wait_bytes(sites_out.at[pl.ds(0, devices - 1)], site_sems.at[0])
    wait_bytes(listed_out.at[pl.ds(0, devices - 1)], site_sems.at[4])

    wait_bytes(returned, site_sems.at[3])
    back = returned[...].reshape(devices, 128)
    by_slot = lax.dot_general(
        back,
        owner_one,
        (((0,), (0,)), ((), ())),
        precision=lax.Precision.HIGHEST,
        preferred_element_type=jnp.float32,
    )
    own = lax.broadcasted_iota(jnp.int32, (128, plants), 0) == slot
    power[...] = kilowatts * 0.001 * jnp.sum(jnp.where(own, by_slot, 0.0), axis=0, keepdims=True)
    sums = jnp.sum(jnp.where(lane[:, 0] == slots, back, 0.0), axis=(0, 1), keepdims=True)
    fleet[...] = jnp.broadcast_to(sums / float(plants * devices), fleet.shape)
    wait_bytes(yields_out.at[pl.ds(0, devices - 1)], site_sems.at[2])
    wait_bytes(placed, done_sem)


def fast_body(
    cloud_field,
    row_gain,
    row_qkv,
    row_out,
    col_gain,
    col_qkv,
    col_out,
    plant_cell,
    plant_decoder_device,
    plant_capacity,
    decode_first,
    decode_second,
):
    rows_here, cols_here, width = cloud_field.shape
    strips = lax.axis_size("strip")
    bands = lax.axis_size("band")
    devices = bands * strips
    length = cols_here * strips
    plants_here = plant_cell.shape[0]

    vmem = pl.BlockSpec(memory_space=pltpu.VMEM)
    anywhere = pl.BlockSpec(memory_space=pl.ANY)
    half = 4 * (width // HEADS)
    bf16 = jnp.bfloat16
    final_field, power, fleet = pl.pallas_call(
        whole_kernel,
        out_shape=(
            jax.ShapeDtypeStruct(cloud_field.shape, bf16),
            jax.ShapeDtypeStruct((1, plants_here), jnp.float32),
            jax.ShapeDtypeStruct((1, 128), jnp.float32),
        ),
        in_specs=[anywhere] + [vmem] * 6 + [anywhere] * 5,
        out_specs=(anywhere, vmem, vmem),
        scratch_shapes=[
            pltpu.VMEM((4, strips, 2, cols_here, width), bf16),
            pltpu.VMEM((width // 128, devices, 32, 128), jnp.float32),
            pltpu.VMEM((2, 2, devices, 16, width), bf16),
            pltpu.VMEM((2, 2, devices, 16, width), bf16),
            pltpu.VMEM((width // 128, 4 * length, 128), jnp.float32),
            pltpu.VMEM((8, bands, length // bands, width), bf16),
            pltpu.VMEM((8, bands, length // bands, width), bf16),
            pltpu.VMEM((8, devices * 8, length), bf16),
            pltpu.VMEM((devices, 16, width // 2), bf16),
            pltpu.VMEM((devices, 16, width // 2), bf16),
            pltpu.VMEM((devices, 1, 128), jnp.float32),
            pltpu.VMEM((devices, 1, 128), jnp.float32),
            pltpu.VMEM((devices, 1, 128), jnp.float32),
            pltpu.VMEM((devices, 1, 128), jnp.float32),
            pltpu.VMEM((width // 128, rows_here * cols_here, 128), jnp.float32),
            pltpu.VMEM(cloud_field.shape, bf16),
            pltpu.VMEM(row_qkv.shape, bf16),
            pltpu.VMEM(row_out.shape, bf16),
            pltpu.VMEM(col_qkv.shape, bf16),
            pltpu.VMEM(col_out.shape, bf16),
            pltpu.VMEM(decode_first.shape, bf16),
            pltpu.VMEM((half, half), bf16),
            pltpu.SemaphoreType.DMA((4,)),
            pltpu.SemaphoreType.DMA((4,)),
            pltpu.SemaphoreType.DMA((2, 2)),
            pltpu.SemaphoreType.DMA((2, 2)),
            pltpu.SemaphoreType.DMA((8,)),
            pltpu.SemaphoreType.DMA((8,)),
            pltpu.SemaphoreType.DMA((6,)),
            pltpu.SemaphoreType.DMA,
            pltpu.SemaphoreType.DMA((5,)),
        ],
        compiler_params=pltpu.CompilerParams(
            collective_id=0, has_side_effects=True, vmem_limit_bytes=56 * 1024 * 1024
        ),
        cost_estimate=pl.CostEstimate(
            flops=4 * rows_here * cols_here * width * (4 * width + 2 * length),
            bytes_accessed=8 * cloud_field.size,
            transcendentals=2 * rows_here * cols_here * HEADS * length,
        ),
    )(
        cloud_field,
        row_gain.reshape(1, width),
        col_gain.reshape(1, width),
        plant_cell.reshape(1, plants_here),
        plant_decoder_device.reshape(1, plants_here),
        plant_capacity.reshape(1, plants_here),
        decode_second,
        row_qkv,
        row_out,
        col_qkv,
        col_out,
        decode_first,
    )
    return (final_field, power[0], fleet[0, 0])


def body(
    cloud_field,
    row_gain,
    row_qkv,
    row_out,
    col_gain,
    col_qkv,
    col_out,
    plant_cell,
    plant_decoder_device,
    plant_capacity,
    decode_first,
    decode_second,
):
    rows_here, cols_here, model_width = cloud_field.shape
    strips = lax.axis_size("strip")
    bands = lax.axis_size("band")
    owner_count = bands * strips
    row_share = rows_here // strips
    col_share = cols_here // bands
    shape_send = (strips, row_share, cols_here, model_width)
    mixed_rows = mix_layer(
        lax.all_to_all(
            cloud_field.reshape(shape_send), "strip", split_axis=0, concat_axis=2, tiled=True
        )[0],
        row_gain,
        row_qkv,
        row_out,
    )[None]
    after_rows = lax.all_to_all(
        mixed_rows, "strip", split_axis=2, concat_axis=0, tiled=True
    ).reshape(rows_here, cols_here, model_width)
    turned = lax.all_to_all(
        after_rows.reshape(rows_here, bands, col_share, model_width),
        "band",
        split_axis=1,
        concat_axis=0,
        tiled=True,
    )[:, 0].transpose(1, 0, 2)
    mixed_cols = mix_layer(turned, col_gain, col_qkv, col_out)
    columns_done = mixed_cols.transpose(1, 0, 2)[:, None]
    final_field = lax.all_to_all(
        columns_done, "band", split_axis=0, concat_axis=1, tiled=True
    ).reshape(rows_here, cols_here, model_width)
    plants_here = plant_cell.shape[0]
    most_slots = 2 * plants_here // owner_count
    flat_field = final_field.reshape(rows_here * cols_here, model_width)
    features = flat_field[plant_cell]
    owners = plant_decoder_device[:, 0]
    one_hot = (owners[:, None] == jnp.arange(owner_count, dtype=jnp.int32)[None, :]).astype(
        jnp.int32
    )
    running = jnp.cumsum(one_hot, axis=0)
    slot_of = jnp.sum(one_hot * (running - 1), axis=1)
    destination = owners * most_slots + slot_of
    send_buffer = (
        jnp.zeros((owner_count * most_slots, model_width), jnp.bfloat16)
        .at[destination]
        .set(features)
    )
    send_buffer = send_buffer.reshape(owner_count, most_slots, model_width)
    hidden = jax.nn.gelu(
        jnp.einsum(
            "smd,dh->smh",
            lax.all_to_all(send_buffer, ("band", "strip"), split_axis=0, concat_axis=0, tiled=True),
            decode_first,
            preferred_element_type=jnp.float32,
        )
    ).astype(jnp.bfloat16)
    output_logit = jnp.einsum(
        "smh,h->sm", hidden, decode_second[0], preferred_element_type=jnp.float32
    )
    yields = jax.nn.softplus(output_logit)
    returned = lax.all_to_all(yields, ("band", "strip"), split_axis=0, concat_axis=0, tiled=True)
    own_yield = returned.reshape(-1)[destination]
    capacity_w = plant_capacity.astype(jnp.float32) * 0.001
    plant_power = capacity_w * own_yield
    power_sum = lax.psum(jnp.sum(plant_power), ("band", "strip"))
    fleet_yield = power_sum / float(plants_here * owner_count)
    return (final_field, plant_power, fleet_yield)


def solution(mesh):
    grid_fits = 32 * mesh.shape["strip"] == 256 and 64 * mesh.shape["band"] == 256
    return jax.shard_map(
        fast_body if grid_fits else body,
        mesh=mesh,
        in_specs=(
            P("band", "strip", None),
            P(),
            P(),
            P(),
            P(),
            P(),
            P(),
            P(("band", "strip")),
            P(("band", "strip"), None),
            P(("band", "strip")),
            P(("band", "strip"), None),
            P(("band", "strip"), None),
        ),
        out_specs=(P("band", "strip", None), P(("band", "strip")), P()),
        check_vma=False,
    )
```
